32 devices in a mesh: mem: 4 (over z), lat: 8 (over y, x, core).
Axes of the slice: x: 2, y: 2, z: 4, core: 2. Of those that a mesh axis runs over, the one named last changes fastest.
Arguments:
- perturbations: bfloat16 [128, 3, 192, 1280], P('mem', None, 'lat'), may hold values from -0.5 to 0.5
- control: float32 [128, 48, 320], P('mem', 'lat'), may hold values from -6 to 6
- innovations: float32 [3, 192, 1280], P(None, 'lat'), may hold values from -6 to 6
- thresholds: float32 [3], replicated, may hold values from 0.4 to 1.5
Outputs:
- weights: float32 [128, 48, 320], P('mem', 'lat')
- increment: float32 [3, 192, 1280], P(None, 'lat', 'mem')
The draws below stay inside these ranges and needn't reach their ends.
All inputs are finite; a program needn't handle non-finite values.
Results may differ from the reference program's by a relative error of at most 0.0003.
Values sent between devices are 32-bit elements; how exact they have to be, the bound alone decides.
No kernel may reach another device: no remote copies, remote signals or barrier semaphores. Data moves between devices by JAX's collectives and lax.ppermute only.
A program may use at most 64 MiB of HBM per device.

```python
import math
import jax
import jax.numpy as jnp
from jax import lax

MEM_DEV = 32
CLON = 320
VARS = 3
RATIO = 4
HALF = 5
STEPS = 2
MEMBERS = 128
NCR = 48
FROWS = 192
FLON = 1280
N_MEM = 4


def block_scale(rng, extent, cuts, smallest, largest):
    def one(position, shards_of):
        draws = jax.random.uniform(jax.random.fold_in(jax.random.fold_in(rng, 6), position), (shards_of,), jnp.float32, smallest / len(cuts), largest / len(cuts))
        return jnp.repeat(jnp.exp(draws), extent[position] // shards_of).reshape((-1,) + (1,) * (len(extent) - position - 1))

    loudness = one(*cuts[0])
    for cut in cuts[1:]:
        loudness = loudness * one(*cut)
    return loudness


def noise(stream_key, shape, spread, bound, pieces=(), kind=jnp.bfloat16):
    values = jax.random.normal(stream_key, shape, jnp.float32) * spread
    if len(pieces) > 0:
        values = block_scale(stream_key, shape, pieces, -0.22, 0.18) * values
    return jnp.clip(values, min=-bound, max=bound).astype(kind)


def setup_inputs(seed: int = 0) -> dict:
    keys = jax.random.split(jax.random.key(seed), 5)
    return {
        "perturbations": noise(keys[0], (MEMBERS, VARS, FROWS, FLON), MEMBERS ** -0.5, 0.5, ((0, 4), (2, 8))),
        "control": noise(keys[1], (MEMBERS, NCR, CLON), 1.0, 6.0, ((0, 4), (1, 8)), jnp.float32),
        "innovations": noise(keys[2], (VARS, FROWS, FLON), 1.0, 6.0, ((1, 8),), jnp.float32),
        "thresholds": jnp.clip(jnp.exp(jax.random.uniform(keys[3], (VARS,), jnp.float32, math.log(0.4), math.log(1.5))), 0.4, 1.5),
    }


def tent_table(fine_count, coarse_count, periodic):
    fine_pos = jnp.arange(fine_count, dtype=jnp.float32)[:, None]
    coarse_pos = jnp.arange(coarse_count, dtype=jnp.float32)[None, :]
    distance = fine_pos + 0.5 - RATIO * coarse_pos - RATIO / 2
    if periodic:
        distance = jnp.mod(distance + fine_count / 2, fine_count) - fine_count / 2
    return jnp.maximum(0.0, 1.0 - jnp.abs(distance) / RATIO)


def smooth_table(count):
    distance = jnp.abs(jnp.arange(count, dtype=jnp.float32)[None, :] - jnp.arange(count, dtype=jnp.float32)[:, None])
    return jnp.where(distance <= HALF, (1.0 - distance / (HALF + 1)) / 2, 0.0)


def reference(perturbations, control, innovations, thresholds):
    highest = lax.Precision.HIGHEST
    smooth = smooth_table(NCR)
    lat_up = tent_table(FROWS, NCR, False)
    lon_up = tent_table(FLON, CLON, True).T
    pert_blocks = perturbations.reshape(N_MEM, MEM_DEV, VARS, FROWS, FLON)

    def forward(weights):
        def add_block(running, blocks):
            pert, group = blocks
            smoothed = jnp.einsum("jq,bqc->bjc", smooth, group, precision=highest)
            rowwise = jnp.einsum("iq,bqc->bic", lat_up, smoothed, precision=highest)
            refined = jnp.einsum("bic,cf->bif", rowwise, lon_up, precision=highest)
            return running + jnp.sum(pert.astype(jnp.float32) * refined[:, None], axis=0), None
        start = jnp.zeros((VARS, FROWS, FLON), jnp.float32)
        result, unused = lax.scan(add_block, start, (pert_blocks, weights.reshape(N_MEM, MEM_DEV, NCR, CLON)))
        return result

    def adjoint(misfit, weights):
        def one_block(blocks):
            pert, group = blocks
            weighted = jnp.sum(pert.astype(jnp.float32) * misfit[None], axis=1)
            columns = jnp.einsum("bif,cf->bic", weighted, lon_up, precision=highest)
            coarse = jnp.einsum("iq,bic->bqc", lat_up, columns, precision=highest)
            return group + jnp.einsum("jq,bqc->bjc", smooth, coarse, precision=highest)
        result = lax.map(one_block, (pert_blocks, weights.reshape(N_MEM, MEM_DEV, NCR, CLON)))
        return result.reshape(MEMBERS, NCR, CLON)

    weights = control
    increment = forward(control)
    for iteration in range(STEPS):
        limit = thresholds[:, None, None]
        misfit = jnp.clip(increment - innovations, -limit, limit)
        gradient = adjoint(misfit, weights)
        image = forward(gradient)
        grad_sq = jnp.sum(gradient * gradient)
        image_sq = jnp.sum(image * image)
        step_len = grad_sq / (grad_sq + image_sq)
        weights = weights - step_len * gradient
        increment = increment - step_len * image
    return weights, increment
```

```python
import functools

import jax
import jax.numpy as jnp
import ml_dtypes
import numpy as np
from jax import lax
from jax.experimental import pallas as pl
from jax.experimental.pallas import tpu as pltpu
from jax.sharding import PartitionSpec as P

RATIO = 4
HALF = 5
STEPS = 2
REACH = HALF + 1
LANES = 128
WIN = 64
MARGIN = 32
FINE = RATIO * WIN
CHUNK = 8
F32 = jnp.float32
BF16 = jnp.bfloat16


def tent(distance):
    return max(0.0, 1.0 - abs(distance) / RATIO)


def smooth(distance):
    return (1.0 - abs(distance) / REACH) / 2 if abs(distance) <= HALF else 0.0


def window_table():
    fine = np.arange(FINE, dtype=np.float64)[None, :]
    coarse = np.arange(LANES, dtype=np.float64)[:, None] - MARGIN
    table = np.maximum(0.0, 1.0 - np.abs(fine + 0.5 - RATIO * coarse - RATIO / 2) / RATIO)
    return table.astype(ml_dtypes.bfloat16)


class Sizes:
    def __init__(self, mesh, perturbations, control):
        self.n_mem = mesh.shape["mem"]
        self.n_lat = mesh.shape["lat"]
        self.members = control.shape[0]
        self.rows = control.shape[1]
        self.cols = control.shape[2]
        self.vars = perturbations.shape[1]
        self.fine_rows = perturbations.shape[2]
        self.fine_cols = perturbations.shape[3]
        assert self.rows == REACH and self.cols % LANES == WIN
        assert self.fine_rows == RATIO * self.rows and self.fine_cols == RATIO * self.cols
        self.windows = self.cols // WIN
        self.ext = self.cols + 2 * MARGIN
        self.slab = self.rows * self.members
        self.full = self.cols // LANES
        self.packed = self.full * self.slab + self.slab // 2
        self.field_rows = self.vars * self.fine_rows
        self.share = self.fine_cols // self.n_mem
        self.share_full = self.share // LANES
        self.share_rem = self.share % LANES
        self.groups = LANES // self.share_rem if self.share_rem else 1
        self.rem_rows = -(-self.field_rows // 8 // self.groups) * 8 if self.share_rem else 0
        self.part_rows = self.share_full * self.field_rows + self.rem_rows


def lane(shape):
    return lax.broadcasted_iota(jnp.int32, shape, 1)


def half_turn(x):
    return pltpu.roll(x, WIN, 1)


def pack_slab(size, first, last, middle):
    rows = size.slab
    at = lane((rows, LANES))
    pieces = list(middle)
    pieces.append(jnp.where(at < LANES - MARGIN, last, first))
    half = rows // 2
    at = lane((half, LANES))
    inner = (at >= MARGIN) & (at < LANES - MARGIN)
    pieces.append(jnp.where(inner, first[:half], half_turn(first[half:])))
    return pieces


def unpack_slab(size, packed):
    rows = size.slab
    middle = [packed[i * rows : (i + 1) * rows] for i in range(size.full - 1)]
    mixed = packed[(size.full - 1) * rows : size.full * rows]
    rest = packed[size.full * rows :]
    rest = jnp.concatenate([rest, half_turn(rest)], axis=0)
    at = lane((rows, LANES))
    first = jnp.where(at < MARGIN, half_turn(mixed), jnp.where(at < LANES - MARGIN, rest, mixed))
    last = jnp.where(at < LANES - MARGIN, mixed, half_turn(rest))
    return [first] + middle + [last]


def tiles_of(ref, count):
    return [ref[:, i * LANES : (i + 1) * LANES] for i in range(count)]


def put_packed(out, pieces):
    at = 0
    for piece in pieces:
        out[at : at + piece.shape[0], :] = piece
        at += piece.shape[0]


def pack_ref(size, out, tiles):
    put_packed(out, pack_slab(size, tiles[0], tiles[-1], tiles[1:-1]))


def place():
    lat = lax.axis_index("lat")
    odd = lax.rem(lat, 2) == 1
    low = (lat > 0).astype(F32)
    high = (lat < lax.axis_size("lat") - 1).astype(F32)
    return odd, low, high


def sides(a, b):
    odd, low, high = place()
    lower = jnp.where(odd, a, b) * low
    upper = jnp.where(odd, b, a) * high
    return lower, upper


def step_length(scal_ref):
    total = jnp.sum(scal_ref[...].reshape(-1, 8, LANES), axis=0)
    grad_sq = total[0:1, 0:1]
    image_sq = total[1:2, 0:1]
    return grad_sq / (grad_sq + image_sq)


def enter_kernel(size, control_ref, own_ref, packed_ref):
    slabs = [control_ref[:, r, :] for r in range(size.rows)]
    x = jnp.concatenate(slabs, axis=0)
    x = jnp.concatenate([x[:, size.cols - MARGIN :], x, x[:, :MARGIN]], axis=1)
    own_ref[...] = x
    pack_ref(size, packed_ref, tiles_of(own_ref, size.ext // LANES))


def forward_kernel(size, own_ref, a_ref, b_ref, pert_ref, table_ref, *rest):
    outs = rest[: size.n_mem]
    ext_ref, coarse_ref, rows_ref, acc_ref, parts_ref = rest[size.n_mem :]
    step = pl.program_id(0)
    members = size.members
    n_tiles = size.ext // LANES
    fine_rows = size.fine_rows

    @pl.when(step == 0)
    def _():
        unused, low, high = place()
        lower, upper = sides(a_ref[...], b_ref[...])
        lower = unpack_slab(size, lower)
        upper = unpack_slab(size, upper)
        n = size.slab
        for e in range(n_tiles):
            cut = slice(e * LANES, (e + 1) * LANES)
            ext_ref[0:n, cut] = lower[e]
            ext_ref[n : 2 * n, cut] = own_ref[:, cut]
            ext_ref[2 * n : 3 * n, cut] = upper[e]
        for e in range(n_tiles):
            cut = slice(e * LANES, (e + 1) * LANES)
            for g in range(0, members, 8):
                held = [
                    ext_ref[k * members + g : k * members + g + 8, cut] for k in range(3 * REACH)
                ]
                for j in range(size.rows + 2):
                    total = None
                    for k in range(3 * REACH):
                        weight = smooth(j - 1 - (k - REACH))
                        if weight:
                            term = held[k] * weight
                            total = term if total is None else total + term
                    if j == 0:
                        total = total * low
                    if j == size.rows + 1:
                        total = total * high
                    coarse_ref[j * members + g : j * members + g + 8, cut] = total
        for t in range(size.windows):
            e = t // 2
            held = []
            for j in range(size.rows + 2):
                at = slice(j * members, (j + 1) * members)
                value = coarse_ref[at, e * LANES : (e + 1) * LANES]
                if t % 2:
                    other = coarse_ref[at, (e + 1) * LANES : (e + 2) * LANES]
                    value = half_turn(jnp.where(lane(value.shape) < WIN, other, value))
                held.append(value)
            for i in range(fine_rows):
                total = None
                for j in range(size.rows + 2):
                    weight = tent(i + 0.5 - RATIO * (j - 1) - RATIO / 2)
                    if weight:
                        term = held[j] * weight
                        total = term if total is None else total + term
                rows_ref[t, pl.ds(i, members, stride=fine_rows), :] = total
        acc_ref[...] = jnp.zeros_like(acc_ref)

    block = CHUNK * fine_rows
    first = pl.multiple_of(step * block, 8)
    for t in range(size.windows):
        x = rows_ref[t, pl.ds(first, block), :]
        head = x.astype(BF16)
        tail = (x - head.astype(F32)).astype(BF16)
        refined = jnp.dot(
            jnp.concatenate([head, tail], axis=1), table_ref[...], preferred_element_type=F32
        )
        cut = slice(t * FINE, (t + 1) * FINE)
        for v in range(size.vars):
            at = slice(v * fine_rows, (v + 1) * fine_rows)
            total = acc_ref[at, cut]
            for m in range(CHUNK):
                total = total + pert_ref[m, v, :, cut].astype(F32) * refined[
                    m * fine_rows : (m + 1) * fine_rows
                ]
            acc_ref[at, cut] = total

    @pl.when(step == pl.num_programs(0) - 1)
    def _():
        for q in range(size.n_mem):
            put_part(size, parts_ref.at[q], acc_ref, q * size.share)
        mine = lax.axis_index("mem")
        for d in range(size.n_mem):
            outs[d][...] = parts_ref[mine ^ d]


def field_tile(acc_ref, start):
    e, shift = start // LANES, start % LANES
    tile = acc_ref[:, e * LANES : (e + 1) * LANES]
    if shift == 0:
        return tile
    if (e + 1) * LANES < acc_ref.shape[1]:
        other = acc_ref[:, (e + 1) * LANES : (e + 2) * LANES]
        tile = jnp.where(lane(tile.shape) < shift, other, tile)
    return pltpu.roll(tile, LANES - shift, 1)


def put_part(size, out, acc_ref, start):
    rows = size.field_rows
    for j in range(size.share_full):
        out[j * rows : (j + 1) * rows, :] = field_tile(acc_ref, start + j * LANES)
    if size.share_rem:
        tile = field_tile(acc_ref, start + size.share_full * LANES)
        tile = jnp.where(lane(tile.shape) < size.share_rem, tile, 0.0)
        missing = size.rem_rows * size.groups - rows
        if missing:
            tile = jnp.concatenate([tile, jnp.zeros((missing, LANES), F32)], axis=0)
        total = None
        for g in range(size.groups):
            term = tile[g * size.rem_rows : (g + 1) * size.rem_rows]
            if g:
                term = pltpu.roll(term, g * size.share_rem, 1)
            total = term if total is None else total + term
        out[size.share_full * rows :, :] = total


def part_tiles(size, part):
    rows = size.field_rows
    tiles = [(part[j * rows : (j + 1) * rows], LANES) for j in range(size.share_full)]
    if size.share_rem:
        rest = part[size.share_full * rows :]
        stack = [rest]
        for g in range(1, size.groups):
            stack.append(pltpu.roll(rest, LANES - g * size.share_rem, 1))
        tiles.append((jnp.concatenate(stack, axis=0)[:rows], size.share_rem))
    return tiles


def total_kernel(count, *refs):
    parts, out_ref = refs[:count], refs[count]
    total = parts[0][...]
    for part in parts[1:]:
        total = total + part[...]
    out_ref[...] = total


def squares_kernel(count, *refs):
    parts, grad_ref, out_ref, scal_ref = refs[:count], refs[count], refs[count + 1], refs[count + 2]
    total = parts[0][...]
    for part in parts[1:]:
        total = total + part[...]
    out_ref[...] = total
    image_sq = jnp.sum(total * total)
    grad = grad_ref[...]
    grad_sq = jnp.sum(grad * grad)
    row = lax.broadcasted_iota(jnp.int32, (8, LANES), 0)
    tile = jnp.where(row == 0, grad_sq, jnp.where(row == 1, image_sq, 0.0))
    for i in range(scal_ref.shape[0] // 8):
        scal_ref[i * 8 : (i + 1) * 8, :] = tile


def adjoint_kernel(size, later, *refs):
    refs = list(refs)
    parts = [refs.pop(0) for i in range(size.n_mem)]
    if later:
        scal_ref = refs.pop(0)
        before_ref = refs.pop(0)
    innov_ref, limit_ref, pert_ref, table_ref = refs[:4]
    refs = refs[4:]
    a_ref, b_ref, own_ref = refs[:3]
    refs = refs[3:]
    if not later:
        field_ref = refs.pop(0)
    misfit_ref, parts_ref, cols_ref, coarse_ref, spread_ref = refs
    step = pl.program_id(0)
    members = size.members
    n_tiles = size.ext // LANES
    fine_rows = size.fine_rows

    @pl.when(step == 0)
    def _():
        mine = lax.axis_index("mem")
        for d in range(size.n_mem):
            parts_ref[mine ^ d] = parts[d][...]
        for q in range(size.n_mem):
            start = q * size.share
            for tile, width in part_tiles(size, parts_ref[q]):
                e, shift = start // LANES, start % LANES
                turned = pltpu.roll(tile, shift, 1) if shift else tile
                at = lane(turned.shape)
                cut = slice(e * LANES, (e + 1) * LANES)
                if shift == 0 and width == LANES:
                    misfit_ref[:, cut] = turned
                else:
                    inside = (at >= shift) & (at < shift + width)
                    misfit_ref[:, cut] = jnp.where(inside, turned, misfit_ref[:, cut])
                if shift + width > LANES:
                    cut = slice((e + 1) * LANES, (e + 2) * LANES)
                    inside = at < shift + width - LANES
                    misfit_ref[:, cut] = jnp.where(inside, turned, misfit_ref[:, cut])
                start += width
        value = misfit_ref[...]
        if later:
            value = before_ref[...] - step_length(scal_ref) * value
        else:
            field_ref[...] = value
        for v in range(size.vars):
            at = slice(v * fine_rows, (v + 1) * fine_rows)
            limit = limit_ref[v]
            misfit_ref[at, :] = jnp.clip(value[at] - innov_ref[v], -limit, limit)

    block = CHUNK * fine_rows
    first = pl.multiple_of(step * block, 8)
    tops = [None] * n_tiles
    for t in range(size.windows):
        cut = slice(t * FINE, (t + 1) * FINE)
        mis = [misfit_ref[v * fine_rows : (v + 1) * fine_rows, cut] for v in range(size.vars)]
        weighted = []
        for m in range(CHUNK):
            total = pert_ref[m, 0, :, cut].astype(F32) * mis[0]
            for v in range(1, size.vars):
                total = total + pert_ref[m, v, :, cut].astype(F32) * mis[v]
            weighted.append(total)
        x = jnp.concatenate(weighted, axis=0)
        head = x.astype(BF16)
        tail = (x - head.astype(F32)).astype(BF16)
        columns = jnp.dot(
            jnp.concatenate([head, tail], axis=1), table_ref[...], preferred_element_type=F32
        )
        e = t // 2
        if t % 2 == 0:
            tops[e] = columns if tops[e] is None else tops[e] + columns
        else:
            turned = half_turn(columns)
            at = lane(turned.shape)
            tops[e] = tops[e] + jnp.where(at >= WIN, turned, 0.0)
            tops[e + 1] = jnp.where(at < WIN, turned, 0.0)
    for e in range(n_tiles):
        cols_ref[e, pl.ds(first, block), :] = tops[e]

    @pl.when(step == pl.num_programs(0) - 1)
    def _():
        odd, low, high = place()
        for e in range(n_tiles):
            cut = slice(e * LANES, (e + 1) * LANES)
            sums = [None] * (size.rows + 2)
            for i in range(fine_rows):
                value = cols_ref[e, pl.ds(i, members, stride=fine_rows), :]
                for j in range(size.rows + 2):
                    weight = tent(i + 0.5 - RATIO * (j - 1) - RATIO / 2)
                    if weight:
                        term = value * weight
                        sums[j] = term if sums[j] is None else sums[j] + term
            sums[0] = sums[0] * low
            sums[-1] = sums[-1] * high
            for j in range(size.rows + 2):
                coarse_ref[j * members : (j + 1) * members, cut] = sums[j]
        head = coarse_ref[:, 0:LANES]
        tail = coarse_ref[:, (n_tiles - 1) * LANES :]
        at = lane(head.shape)
        turned_head, turned_tail = half_turn(head), half_turn(tail)
        coarse_ref[:, 0:LANES] = head + jnp.where(at < WIN, turned_tail, 0.0)
        coarse_ref[:, (n_tiles - 1) * LANES :] = tail + jnp.where(at >= WIN, turned_head, 0.0)
        for e in range(n_tiles):
            cut = slice(e * LANES, (e + 1) * LANES)
            for g in range(0, members, 8):
                held = [
                    coarse_ref[j * members + g : j * members + g + 8, cut]
                    for j in range(size.rows + 2)
                ]
                for k in range(3 * REACH):
                    total = None
                    for j in range(size.rows + 2):
                        weight = smooth(j - 1 - (k - REACH))
                        if weight:
                            term = held[j] * weight
                            total = term if total is None else total + term
                    spread_ref[k * members + g : k * members + g + 8, cut] = total
        n = size.slab

        def packed_of(part):
            tiles = [
                spread_ref[part * n : (part + 1) * n, e * LANES : (e + 1) * LANES]
                for e in range(n_tiles)
            ]
            return pack_slab(size, tiles[0], tiles[-1], tiles[1:-1])

        lower, upper = packed_of(0), packed_of(2)
        own_ref[...] = spread_ref[n : 2 * n, :]
        put_packed(a_ref, [jnp.where(odd, x, y) for x, y in zip(lower, upper)])
        put_packed(b_ref, [jnp.where(odd, y, x) for x, y in zip(lower, upper)])


def gradient_kernel(size, later, *refs):
    refs = list(refs)
    own_ref, a_ref, b_ref, weights_ref = refs[:4]
    refs = refs[4:]
    weights = weights_ref[...]
    if later:
        scal_ref, before_ref = refs.pop(0), refs.pop(0)
        weights = weights - step_length(scal_ref) * before_ref[...]
    grad_ref, packed_ref = refs[:2]
    if later:
        refs[2][...] = weights
    lower, upper = sides(a_ref[...], b_ref[...])
    arrived = unpack_slab(size, lower + upper)
    for e in range(size.ext // LANES):
        cut = slice(e * LANES, (e + 1) * LANES)
        grad_ref[:, cut] = weights[:, cut] + own_ref[:, cut] + arrived[e]
    pack_ref(size, packed_ref, tiles_of(grad_ref, size.ext // LANES))


def leave_kernel(size, weights_ref, grad_ref, field_ref, image0_ref, scal0_ref, image1_ref,
                 scal1_ref, out_weights_ref, out_field_ref):
    second = step_length(scal1_ref)
    weights = weights_ref[...] - second * grad_ref[...]
    n_tiles = size.ext // LANES
    tiles = [weights[:, e * LANES : (e + 1) * LANES] for e in range(n_tiles)]
    for e in range(n_tiles):
        tile = tiles[e]
        if e + 1 < n_tiles:
            tile = jnp.where(lane(tile.shape) < MARGIN, tiles[e + 1], tile)
        tile = pltpu.roll(tile, LANES - MARGIN, 1)
        start = e * LANES
        width = min(LANES, size.cols - start)
        for r in range(size.rows):
            rows = slice(r * size.members, (r + 1) * size.members)
            out_weights_ref[:, r, start : start + width] = tile[rows, :width]
    field = field_ref[...] - step_length(scal0_ref) * image0_ref[...] - second * image1_ref[...]
    start = 0
    for tile, width in part_tiles(size, field):
        for v in range(size.vars):
            rows = slice(v * size.fine_rows, (v + 1) * size.fine_rows)
            out_field_ref[v, :, start : start + width] = tile[rows, :width]
        start += width


def whole():
    return pl.BlockSpec(memory_space=pltpu.VMEM)


def params():
    return pltpu.CompilerParams(vmem_limit_bytes=24 * 1024 * 1024)


def array(*shape):
    return jax.ShapeDtypeStruct(shape, F32)


def call(kernel, outs, *args):
    return pl.pallas_call(
        kernel,
        out_shape=outs,
        in_specs=[whole()] * len(args),
        out_specs=jax.tree.map(lambda unused: whole(), outs),
        compiler_params=params(),
    )(*args)


def per_device(mesh, perturbations, control, innovations, thresholds):
    size = Sizes(mesh, perturbations, control)
    n_mem, n_lat, members = size.n_mem, size.n_lat, size.members
    devices = n_mem * n_lat
    table = window_table()
    up_table = jnp.asarray(np.concatenate([table, table], axis=0))
    down_table = jnp.asarray(np.concatenate([table.T, table.T], axis=0))
    pairs = [(i, i ^ 1) for i in range(n_lat)]
    cross = [(i, (i - 1 if i % 2 == 0 else i + 1) % n_lat) for i in range(n_lat)]
    steps = members // CHUNK
    slab = array(size.slab, size.ext)
    packed = array(size.packed, LANES)
    part = array(size.part_rows, LANES)
    scal = array(devices * 8, LANES)

    def same(*shape):
        return pl.BlockSpec(shape, lambda i: (0,) * len(shape))

    pert_spec = pl.BlockSpec(
        (CHUNK, size.vars, size.fine_rows, size.fine_cols), lambda i: (i, 0, 0, 0)
    )

    def swap(to_a, to_b):
        return lax.ppermute(to_a, "lat", pairs), lax.ppermute(to_b, "lat", cross)

    def between(parts, d):
        return lax.ppermute(parts, "mem", [(i, i ^ d) for i in range(n_mem)])

    far_first = sorted(range(1, n_mem), key=lambda d: -d)

    def reduced(outs):
        moved = {d: between(outs[d], d) for d in far_first}
        return [outs[0]] + [moved[d] for d in range(1, n_mem)]

    def gathered(own):
        moved = {d: between(own, d) for d in far_first}
        return [own] + [moved[d] for d in range(1, n_mem)]

    def forward(own, a, b):
        return pl.pallas_call(
            functools.partial(forward_kernel, size),
            grid=(steps,),
            out_shape=[part] * n_mem,
            in_specs=[
                same(size.slab, size.ext),
                same(size.packed, LANES),
                same(size.packed, LANES),
                pert_spec,
                same(2 * LANES, FINE),
            ],
            out_specs=[same(size.part_rows, LANES)] * n_mem,
            scratch_shapes=[
                pltpu.VMEM((3 * size.slab, size.ext), F32),
                pltpu.VMEM(((size.rows + 2) * members, size.ext), F32),
                pltpu.VMEM((size.windows, members * size.fine_rows, LANES), F32),
                pltpu.VMEM((size.field_rows, size.fine_cols), F32),
                pltpu.VMEM((n_mem, size.part_rows, LANES), F32),
            ],
            compiler_params=params(),
        )(own, a, b, perturbations, up_table)

    def adjoint(parts, scal_all=None, before=None):
        later = scal_all is not None
        field = array(size.field_rows, size.fine_cols)
        outs = [packed, packed, slab] + ([] if later else [field])
        out_specs = [
            same(size.packed, LANES),
            same(size.packed, LANES),
            same(size.slab, size.ext),
        ] + ([] if later else [same(size.field_rows, size.fine_cols)])
        args = list(parts)
        in_specs = [same(size.part_rows, LANES)] * n_mem
        if later:
            args += [scal_all, before]
            in_specs += [same(devices * 8, LANES), same(size.field_rows, size.fine_cols)]
        args += [innovations, thresholds, perturbations, down_table]
        in_specs += [
            same(size.vars, size.fine_rows, size.fine_cols),
            pl.BlockSpec(memory_space=pltpu.SMEM),
            pert_spec,
            same(2 * FINE, LANES),
        ]
        n_tiles = size.ext // LANES
        return pl.pallas_call(
            functools.partial(adjoint_kernel, size, later),
            grid=(steps,),
            out_shape=outs,
            in_specs=in_specs,
            out_specs=out_specs,
            scratch_shapes=[
                pltpu.VMEM((size.field_rows, size.fine_cols), F32),
                pltpu.VMEM((n_mem, size.part_rows, LANES), F32),
                pltpu.VMEM((n_tiles, members * size.fine_rows, LANES), F32),
                pltpu.VMEM(((size.rows + 2) * members, size.ext), F32),
                pltpu.VMEM((3 * size.slab, size.ext), F32),
            ],
            compiler_params=params(),
        )(*args)

    def everywhere(tile):
        moved = lax.all_to_all(tile.reshape(devices, 8, LANES), ("mem", "lat"), 0, 0)
        return moved.reshape(devices * 8, LANES)

    own, sent = call(functools.partial(enter_kernel, size), [slab, packed], control)
    parts = reduced(forward(own, *swap(sent, sent)))
    field0 = call(functools.partial(total_kernel, n_mem), part, *parts)
    to_a, to_b, spread, field_all = adjoint(gathered(field0))
    grad0, sent = call(
        functools.partial(gradient_kernel, size, False),
        [slab, packed],
        spread,
        *swap(to_a, to_b),
        own,
    )
    parts = reduced(forward(grad0, *swap(sent, sent)))
    image0, scal0 = call(
        functools.partial(squares_kernel, n_mem), [part, scal], *parts, sent
    )
    images = gathered(image0)
    scal0 = everywhere(scal0)
    to_a, to_b, spread = adjoint(images, scal0, field_all)
    grad1, sent, weights1 = call(
        functools.partial(gradient_kernel, size, True),
        [slab, packed, slab],
        spread,
        *swap(to_a, to_b),
        own,
        scal0,
        grad0,
    )
    parts = reduced(forward(grad1, *swap(sent, sent)))
    image1, scal1 = call(
        functools.partial(squares_kernel, n_mem), [part, scal], *parts, sent
    )
    scal1 = everywhere(scal1)
    return tuple(
        call(
            functools.partial(leave_kernel, size),
            [
                array(members, size.rows, size.cols),
                array(size.vars, size.fine_rows, size.share),
            ],
            weights1,
            grad1,
            field0,
            image0,
            scal0,
            image1,
            scal1,
        )
    )


def solution(mesh):
    return jax.shard_map(
        functools.partial(per_device, mesh),
        mesh=mesh,
        in_specs=(P("mem", None, "lat", None), P("mem", "lat", None), P(None, "lat", None), P()),
        out_specs=(P("mem", "lat", None), P(None, "lat", "mem")),
        check_vma=False,
    )
```

```python
import functools

import jax
import jax.numpy as jnp
import ml_dtypes
import numpy as np
from jax import lax
from jax.experimental import pallas as pl
from jax.experimental.pallas import tpu as pltpu
from jax.sharding import PartitionSpec as P

RATIO = 4
HALF = 5
STEPS = 2
REACH = HALF + 1
LANES = 128
WIN = 64
MARGIN = 32
FINE = RATIO * WIN
CHUNK = 8
F32 = jnp.float32
BF16 = jnp.bfloat16


def tent(distance):
    return max(0.0, 1.0 - abs(distance) / RATIO)


def smooth(distance):
    return (1.0 - abs(distance) / REACH) / 2 if abs(distance) <= HALF else 0.0


def window_table():
    fine = np.arange(FINE, dtype=np.float64)[None, :]
    coarse = np.arange(LANES, dtype=np.float64)[:, None] - MARGIN
    table = np.maximum(0.0, 1.0 - np.abs(fine + 0.5 - RATIO * coarse - RATIO / 2) / RATIO)
    return table.astype(ml_dtypes.bfloat16)


class Sizes:
    def __init__(self, mesh, perturbations, control):
        self.n_mem = mesh.shape["mem"]
        self.n_lat = mesh.shape["lat"]
        self.members = control.shape[0]
        self.rows = control.shape[1]
        self.cols = control.shape[2]
        self.vars = perturbations.shape[1]
        self.fine_rows = perturbations.shape[2]
        self.fine_cols = perturbations.shape[3]
        assert self.rows == REACH and self.cols % LANES == WIN
        assert self.fine_rows == RATIO * self.rows and self.fine_cols == RATIO * self.cols
        self.windows = self.cols // WIN
        self.ext = self.cols + 2 * MARGIN
        self.slab = self.rows * self.members
        self.full = self.cols // LANES
        self.packed = self.full * self.slab + self.slab // 2
        self.field_rows = self.vars * self.fine_rows
        self.share = self.fine_cols // self.n_mem
        self.share_full = self.share // LANES
        self.share_rem = self.share % LANES
        self.groups = LANES // self.share_rem if self.share_rem else 1
        self.rem_rows = -(-self.field_rows // 8 // self.groups) * 8 if self.share_rem else 0
        self.part_rows = self.share_full * self.field_rows + self.rem_rows


def lane(shape):
    return lax.broadcasted_iota(jnp.int32, shape, 1)


def half_turn(x):
    return pltpu.roll(x, WIN, 1)


def pack_slab(size, first, last, middle):
    rows = size.slab
    at = lane((rows, LANES))
    pieces = list(middle)
    pieces.append(jnp.where(at < LANES - MARGIN, last, first))
    half = rows // 2
    at = lane((half, LANES))
    inner = (at >= MARGIN) & (at < LANES - MARGIN)
    pieces.append(jnp.where(inner, first[:half], half_turn(first[half:])))
    return pieces


def unpack_slab(size, packed):
    rows = size.slab
    middle = [packed[i * rows : (i + 1) * rows] for i in range(size.full - 1)]
    mixed = packed[(size.full - 1) * rows : size.full * rows]
    rest = packed[size.full * rows :]
    rest = jnp.concatenate([rest, half_turn(rest)], axis=0)
    at = lane((rows, LANES))
    first = jnp.where(at < MARGIN, half_turn(mixed), jnp.where(at < LANES - MARGIN, rest, mixed))
    last = jnp.where(at < LANES - MARGIN, mixed, half_turn(rest))
    return [first] + middle + [last]


def tiles_of(ref, count):
    return [ref[:, i * LANES : (i + 1) * LANES] for i in range(count)]


def put_packed(out, pieces):
    at = 0
    for piece in pieces:
        out[at : at + piece.shape[0], :] = piece
        at += piece.shape[0]


def pack_ref(size, out, tiles):
    put_packed(out, pack_slab(size, tiles[0], tiles[-1], tiles[1:-1]))


def place():
    lat = lax.axis_index("lat")
    odd = lax.rem(lat, 2) == 1
    low = (lat > 0).astype(F32)
    high = (lat < lax.axis_size("lat") - 1).astype(F32)
    return odd, low, high


def sides(a, b):
    odd, low, high = place()
    lower = jnp.where(odd, a, b) * low
    upper = jnp.where(odd, b, a) * high
    return lower, upper


def step_length(scal_ref):
    total = jnp.sum(scal_ref[...], axis=0, keepdims=True)
    at = lane(total.shape)
    grad_sq = jnp.sum(jnp.where(at == 0, total, 0.0), axis=1, keepdims=True)
    image_sq = jnp.sum(jnp.where(at == 1, total, 0.0), axis=1, keepdims=True)
    return grad_sq / (grad_sq + image_sq)


def enter_kernel(size, control_ref, own_ref, packed_ref):
    x = control_ref[...]
    x = jnp.concatenate([x[:, size.cols - MARGIN :], x, x[:, :MARGIN]], axis=1)
    own_ref[...] = x
    pack_ref(size, packed_ref, tiles_of(own_ref, size.ext // LANES))


def forward_kernel(size, own_ref, a_ref, b_ref, pert_ref, table_ref, *rest):
    outs = rest[: size.n_mem]
    ext_ref, coarse_ref, rows_ref, acc_ref, parts_ref = rest[size.n_mem :]
    members = size.members
    n_tiles = size.ext // LANES
    fine_rows = size.fine_rows

    unused, low, high = place()
    lower, upper = sides(a_ref[...], b_ref[...])
    lower = unpack_slab(size, lower)
    upper = unpack_slab(size, upper)
    n = size.slab
    for e in range(n_tiles):
        cut = slice(e * LANES, (e + 1) * LANES)
        ext_ref[0:n, cut] = lower[e]
        ext_ref[n : 2 * n, cut] = own_ref[:, cut]
        ext_ref[2 * n : 3 * n, cut] = upper[e]
    for e in range(n_tiles):
        cut = slice(e * LANES, (e + 1) * LANES)
        for g in range(0, members, 8):
            held = [
                ext_ref[k * members + g : k * members + g + 8, cut] for k in range(3 * REACH)
            ]
            for j in range(size.rows + 2):
                total = None
                for k in range(3 * REACH):
                    weight = smooth(j - 1 - (k - REACH))
                    if weight:
                        term = held[k] * weight
                        total = term if total is None else total + term
                if j == 0:
                    total = total * low
                if j == size.rows + 1:
                    total = total * high
                coarse_ref[j * members + g : j * members + g + 8, cut] = total
    for t in range(size.windows):
        e = t // 2
        held = []
        for j in range(size.rows + 2):
            at = slice(j * members, (j + 1) * members)
            value = coarse_ref[at, e * LANES : (e + 1) * LANES]
            if t % 2:
                other = coarse_ref[at, (e + 1) * LANES : (e + 2) * LANES]
                value = half_turn(jnp.where(lane(value.shape) < WIN, other, value))
            held.append(value)
        for i in range(fine_rows):
            total = None
            for j in range(size.rows + 2):
                weight = tent(i + 0.5 - RATIO * (j - 1) - RATIO / 2)
                if weight:
                    term = held[j] * weight
                    total = term if total is None else total + term
            rows_ref[t, pl.ds(i, members, stride=fine_rows), :] = total
    acc_ref[...] = jnp.zeros_like(acc_ref)
    block = CHUNK * fine_rows

    def chunk(step, unused):
        first = pl.multiple_of(step * block, 8)
        for t in range(size.windows):
            x = rows_ref[t, pl.ds(first, block), :]
            head = x.astype(BF16)
            tail = (x - head.astype(F32)).astype(BF16)
            refined = jnp.dot(
                jnp.concatenate([head, tail], axis=1), table_ref[...], preferred_element_type=F32
            )
            cut = slice(t * FINE, (t + 1) * FINE)
            for v in range(size.vars):
                at = slice(v * fine_rows, (v + 1) * fine_rows)
                total = acc_ref[at, cut]
                for m in range(CHUNK):
                    total = total + pert_ref[step * CHUNK + m, v, :, cut].astype(F32) * refined[
                        m * fine_rows : (m + 1) * fine_rows
                    ]
                acc_ref[at, cut] = total
        return unused

    lax.fori_loop(0, members // CHUNK, chunk, 0)
    for q in range(size.n_mem):
        put_part(size, parts_ref.at[q], acc_ref, q * size.share)
    mine = lax.axis_index("mem")
    for d in range(size.n_mem):
        outs[d][...] = parts_ref[mine ^ d]


def field_tile(acc_ref, start):
    e, shift = start // LANES, start % LANES
    tile = acc_ref[:, e * LANES : (e + 1) * LANES]
    if shift == 0:
        return tile
    if (e + 1) * LANES < acc_ref.shape[1]:
        other = acc_ref[:, (e + 1) * LANES : (e + 2) * LANES]
        tile = jnp.where(lane(tile.shape) < shift, other, tile)
    return pltpu.roll(tile, LANES - shift, 1)


def put_part(size, out, acc_ref, start):
    rows = size.field_rows
    for j in range(size.share_full):
        out[j * rows : (j + 1) * rows, :] = field_tile(acc_ref, start + j * LANES)
    if size.share_rem:
        tile = field_tile(acc_ref, start + size.share_full * LANES)
        tile = jnp.where(lane(tile.shape) < size.share_rem, tile, 0.0)
        missing = size.rem_rows * size.groups - rows
        if missing:
            tile = jnp.concatenate([tile, jnp.zeros((missing, LANES), F32)], axis=0)
        total = None
        for g in range(size.groups):
            term = tile[g * size.rem_rows : (g + 1) * size.rem_rows]
            if g:
                term = pltpu.roll(term, g * size.share_rem, 1)
            total = term if total is None else total + term
        out[size.share_full * rows :, :] = total


def part_tiles(size, part):
    rows = size.field_rows
    tiles = [(part[j * rows : (j + 1) * rows], LANES) for j in range(size.share_full)]
    if size.share_rem:
        rest = part[size.share_full * rows :]
        stack = [rest]
        for g in range(1, size.groups):
            stack.append(pltpu.roll(rest, LANES - g * size.share_rem, 1))
        tiles.append((jnp.concatenate(stack, axis=0)[:rows], size.share_rem))
    return tiles


def total_kernel(count, *refs):
    parts, out_ref = refs[:count], refs[count]
    total = parts[0][...]
    for part in parts[1:]:
        total = total + part[...]
    out_ref[...] = total


def squares_kernel(count, *refs):
    parts, grad_ref, out_ref, scal_ref = refs[:count], refs[count], refs[count + 1], refs[count + 2]
    total = parts[0][...]
    for part in parts[1:]:
        total = total + part[...]
    out_ref[...] = total
    image_sq = jnp.sum(total * total)
    grad = grad_ref[...]
    grad_sq = jnp.sum(grad * grad)
    at = lane(scal_ref.shape)
    scal_ref[...] = jnp.where(at == 0, grad_sq, jnp.where(at == 1, image_sq, 0.0))


def adjoint_kernel(size, later, *refs):
    refs = list(refs)
    parts = [refs.pop(0) for i in range(size.n_mem)]
    if later:
        scal_ref = refs.pop(0)
        before_ref = refs.pop(0)
    innov_ref, limit_ref, pert_ref, table_ref = refs[:4]
    refs = refs[4:]
    a_ref, b_ref, own_ref = refs[:3]
    refs = refs[3:]
    if not later:
        field_ref = refs.pop(0)
    misfit_ref, parts_ref, cols_ref, coarse_ref, spread_ref = refs
    members = size.members
    n_tiles = size.ext // LANES
    fine_rows = size.fine_rows

    mine = lax.axis_index("mem")
    for d in range(size.n_mem):
        parts_ref[mine ^ d] = parts[d][...]
    for q in range(size.n_mem):
        start = q * size.share
        for tile, width in part_tiles(size, parts_ref[q]):
            e, shift = start // LANES, start % LANES
            turned = pltpu.roll(tile, shift, 1) if shift else tile
            at = lane(turned.shape)
            cut = slice(e * LANES, (e + 1) * LANES)
            if shift == 0 and width == LANES:
                misfit_ref[:, cut] = turned
            else:
                inside = (at >= shift) & (at < shift + width)
                misfit_ref[:, cut] = jnp.where(inside, turned, misfit_ref[:, cut])
            if shift + width > LANES:
                cut = slice((e + 1) * LANES, (e + 2) * LANES)
                inside = at < shift + width - LANES
                misfit_ref[:, cut] = jnp.where(inside, turned, misfit_ref[:, cut])
            start += width
    value = misfit_ref[...]
    if later:
        value = before_ref[...] - step_length(scal_ref) * value
    else:
        field_ref[...] = value
    for v in range(size.vars):
        at = slice(v * fine_rows, (v + 1) * fine_rows)
        limit = limit_ref[v]
        misfit_ref[at, :] = jnp.clip(value[at] - innov_ref[v], -limit, limit)
    block = CHUNK * fine_rows

    def chunk(step, unused):
        first = pl.multiple_of(step * block, 8)
        tops = [None] * n_tiles
        for t in range(size.windows):
            cut = slice(t * FINE, (t + 1) * FINE)
            mis = [misfit_ref[v * fine_rows : (v + 1) * fine_rows, cut] for v in range(size.vars)]
            weighted = []
            for m in range(CHUNK):
                total = pert_ref[step * CHUNK + m, 0, :, cut].astype(F32) * mis[0]
                for v in range(1, size.vars):
                    total = total + pert_ref[step * CHUNK + m, v, :, cut].astype(F32) * mis[v]
                weighted.append(total)
            x = jnp.concatenate(weighted, axis=0)
            head = x.astype(BF16)
            tail = (x - head.astype(F32)).astype(BF16)
            columns = jnp.dot(
                jnp.concatenate([head, tail], axis=1), table_ref[...], preferred_element_type=F32
            )
            e = t // 2
            if t % 2 == 0:
                tops[e] = columns if tops[e] is None else tops[e] + columns
            else:
                turned = half_turn(columns)
                at = lane(turned.shape)
                tops[e] = tops[e] + jnp.where(at >= WIN, turned, 0.0)
                tops[e + 1] = jnp.where(at < WIN, turned, 0.0)
        for e in range(n_tiles):
            cols_ref[e, pl.ds(first, block), :] = tops[e]
        return unused

    lax.fori_loop(0, members // CHUNK, chunk, 0)
    odd, low, high = place()
    for e in range(n_tiles):
        cut = slice(e * LANES, (e + 1) * LANES)
        sums = [None] * (size.rows + 2)
        for i in range(fine_rows):
            value = cols_ref[e, pl.ds(i, members, stride=fine_rows), :]
            for j in range(size.rows + 2):
                weight = tent(i + 0.5 - RATIO * (j - 1) - RATIO / 2)
                if weight:
                    term = value * weight
                    sums[j] = term if sums[j] is None else sums[j] + term
        sums[0] = sums[0] * low
        sums[-1] = sums[-1] * high
        for j in range(size.rows + 2):
            coarse_ref[j * members : (j + 1) * members, cut] = sums[j]
    head = coarse_ref[:, 0:LANES]
    tail = coarse_ref[:, (n_tiles - 1) * LANES :]
    at = lane(head.shape)
    turned_head, turned_tail = half_turn(head), half_turn(tail)
    coarse_ref[:, 0:LANES] = head + jnp.where(at < WIN, turned_tail, 0.0)
    coarse_ref[:, (n_tiles - 1) * LANES :] = tail + jnp.where(at >= WIN, turned_head, 0.0)
    for e in range(n_tiles):
        cut = slice(e * LANES, (e + 1) * LANES)
        for g in range(0, members, 8):
            held = [
                coarse_ref[j * members + g : j * members + g + 8, cut]
                for j in range(size.rows + 2)
            ]
            for k in range(3 * REACH):
                total = None
                for j in range(size.rows + 2):
                    weight = smooth(j - 1 - (k - REACH))
                    if weight:
                        term = held[j] * weight
                        total = term if total is None else total + term
                spread_ref[k * members + g : k * members + g + 8, cut] = total
    n = size.slab

    def packed_of(part):
        tiles = [
            spread_ref[part * n : (part + 1) * n, e * LANES : (e + 1) * LANES]
            for e in range(n_tiles)
        ]
        return pack_slab(size, tiles[0], tiles[-1], tiles[1:-1])

    lower, upper = packed_of(0), packed_of(2)
    own_ref[...] = spread_ref[n : 2 * n, :]
    put_packed(a_ref, [jnp.where(odd, x, y) for x, y in zip(lower, upper)])
    put_packed(b_ref, [jnp.where(odd, y, x) for x, y in zip(lower, upper)])


def gradient_kernel(size, later, *refs):
    refs = list(refs)
    own_ref, a_ref, b_ref, weights_ref = refs[:4]
    refs = refs[4:]
    weights = weights_ref[...]
    if later:
        scal_ref, before_ref = refs.pop(0), refs.pop(0)
        weights = weights - step_length(scal_ref) * before_ref[...]
    grad_ref, packed_ref = refs[:2]
    if later:
        refs[2][...] = weights
    lower, upper = sides(a_ref[...], b_ref[...])
    arrived = unpack_slab(size, lower + upper)
    for e in range(size.ext // LANES):
        cut = slice(e * LANES, (e + 1) * LANES)
        grad_ref[:, cut] = weights[:, cut] + own_ref[:, cut] + arrived[e]
    pack_ref(size, packed_ref, tiles_of(grad_ref, size.ext // LANES))


def leave_kernel(size, weights_ref, grad_ref, field_ref, image0_ref, scal0_ref, image1_ref,
                 scal1_ref, out_weights_ref, out_field_ref):
    second = step_length(scal1_ref)
    weights = weights_ref[...] - second * grad_ref[...]
    n_tiles = size.ext // LANES
    tiles = [weights[:, e * LANES : (e + 1) * LANES] for e in range(n_tiles)]
    for e in range(n_tiles):
        tile = tiles[e]
        if e + 1 < n_tiles:
            tile = jnp.where(lane(tile.shape) < MARGIN, tiles[e + 1], tile)
        tile = pltpu.roll(tile, LANES - MARGIN, 1)
        start = e * LANES
        width = min(LANES, size.cols - start)
        out_weights_ref[:, start : start + width] = tile[:, :width]
    field = field_ref[...] - step_length(scal0_ref) * image0_ref[...] - second * image1_ref[...]
    start = 0
    for tile, width in part_tiles(size, field):
        for v in range(size.vars):
            rows = slice(v * size.fine_rows, (v + 1) * size.fine_rows)
            out_field_ref[v, :, start : start + width] = tile[rows, :width]
        start += width


def whole():
    return pl.BlockSpec(memory_space=pltpu.VMEM)


def params():
    return pltpu.CompilerParams(vmem_limit_bytes=24 * 1024 * 1024)


def array(*shape):
    return jax.ShapeDtypeStruct(shape, F32)


def call(kernel, outs, *args, scratch=()):
    return pl.pallas_call(
        kernel,
        out_shape=outs,
        in_specs=[
            pl.BlockSpec(memory_space=pltpu.SMEM) if arg.ndim == 1 else whole() for arg in args
        ],
        out_specs=jax.tree.map(lambda unused: whole(), outs),
        scratch_shapes=scratch,
        compiler_params=params(),
    )(*args)


def per_device(mesh, perturbations, control, innovations, thresholds):
    size = Sizes(mesh, perturbations, control)
    n_mem, n_lat, members = size.n_mem, size.n_lat, size.members
    devices = n_mem * n_lat
    table = window_table()
    up_table = jnp.asarray(np.concatenate([table, table], axis=0))
    down_table = jnp.asarray(np.concatenate([table.T, table.T], axis=0))
    pairs = [(i, i ^ 1) for i in range(n_lat)]
    cross = [(i, (i - 1 if i % 2 == 0 else i + 1) % n_lat) for i in range(n_lat)]
    slab = array(size.slab, size.ext)
    packed = array(size.packed, LANES)
    part = array(size.part_rows, LANES)
    scal = array(devices, LANES)

    def swap(to_a, to_b):
        return lax.ppermute(to_a, "lat", pairs), lax.ppermute(to_b, "lat", cross)

    def between(parts, d):
        return lax.ppermute(parts, "mem", [(i, i ^ d) for i in range(n_mem)])

    far_first = sorted(range(1, n_mem), key=lambda d: -d)

    def reduced(outs):
        moved = {d: between(outs[d], d) for d in far_first}
        return [outs[0]] + [moved[d] for d in range(1, n_mem)]

    def gathered(own):
        moved = {d: between(own, d) for d in far_first}
        return [own] + [moved[d] for d in range(1, n_mem)]

    def forward(own, a, b):
        return call(
            functools.partial(forward_kernel, size),
            [part] * n_mem,
            own,
            a,
            b,
            perturbations,
            up_table,
            scratch=[
                pltpu.VMEM((3 * size.slab, size.ext), F32),
                pltpu.VMEM(((size.rows + 2) * members, size.ext), F32),
                pltpu.VMEM((size.windows, members * size.fine_rows, LANES), F32),
                pltpu.VMEM((size.field_rows, size.fine_cols), F32),
                pltpu.VMEM((n_mem, size.part_rows, LANES), F32),
            ],
        )

    def adjoint(parts, *step):
        later = len(step) > 0
        field = array(size.field_rows, size.fine_cols)
        n_tiles = size.ext // LANES
        return call(
            functools.partial(adjoint_kernel, size, later),
            [packed, packed, slab] + ([] if later else [field]),
            *parts,
            *step,
            innovations,
            thresholds,
            perturbations,
            down_table,
            scratch=[
                pltpu.VMEM((size.field_rows, size.fine_cols), F32),
                pltpu.VMEM((n_mem, size.part_rows, LANES), F32),
                pltpu.VMEM((n_tiles, members * size.fine_rows, LANES), F32),
                pltpu.VMEM(((size.rows + 2) * members, size.ext), F32),
                pltpu.VMEM((3 * size.slab, size.ext), F32),
            ],
        )

    def everywhere(tile):
        moved = lax.all_to_all(tile.reshape(devices, 1, LANES), ("mem", "lat"), 0, 0)
        return moved.reshape(devices, LANES)

    own, sent = call(functools.partial(enter_kernel, size), [slab, packed],
        control.transpose(1, 0, 2).reshape(size.slab, size.cols))
    parts = reduced(forward(own, *swap(sent, sent)))
    field0 = call(functools.partial(total_kernel, n_mem), part, *parts)
    to_a, to_b, spread, field_all = adjoint(gathered(field0))
    grad0, sent = call(
        functools.partial(gradient_kernel, size, False),
        [slab, packed],
        spread,
        *swap(to_a, to_b),
        own,
    )
    parts = reduced(forward(grad0, *swap(sent, sent)))
    image0, scal0 = call(
        functools.partial(squares_kernel, n_mem), [part, scal], *parts, sent
    )
    images = gathered(image0)
    scal0 = everywhere(scal0)
    to_a, to_b, spread = adjoint(images, scal0, field_all)
    grad1, sent, weights1 = call(
        functools.partial(gradient_kernel, size, True),
        [slab, packed, slab],
        spread,
        *swap(to_a, to_b),
        own,
        scal0,
        grad0,
    )
    parts = reduced(forward(grad1, *swap(sent, sent)))
    image1, scal1 = call(
        functools.partial(squares_kernel, n_mem), [part, scal], *parts, sent
    )
    scal1 = everywhere(scal1)
    weights, field = call(
        functools.partial(leave_kernel, size),
        [array(size.slab, size.cols), array(size.vars, size.fine_rows, size.share)],
        weights1,
        grad1,
        field0,
        image0,
        scal0,
        image1,
        scal1,
    )
    return weights.reshape(size.rows, members, size.cols).transpose(1, 0, 2), field


def solution(mesh):
    return jax.shard_map(
        functools.partial(per_device, mesh),
        mesh=mesh,
        in_specs=(P("mem", None, "lat", None), P("mem", "lat", None), P(None, "lat", None), P()),
        out_specs=(P("mem", "lat", None), P(None, "lat", "mem")),
        check_vma=False,
    )
```

```python
import functools

import jax
import jax.numpy as jnp
from jax import lax
from jax.experimental import pallas as pl
from jax.experimental.pallas import tpu as pltpu
from jax.sharding import PartitionSpec as P

RATIO = 4
HALF = 5
STEPS = 2
REACH = HALF + 1
LANES = 128
WIN = 64
MARGIN = 32
FINE = RATIO * WIN
CHUNK = 16
GROUPS = 2
F32 = jnp.float32
BF16 = jnp.bfloat16


def tent(distance):
    return max(0.0, 1.0 - abs(distance) / RATIO)


def smooth(distance):
    return (1.0 - abs(distance) / REACH) / 2 if abs(distance) <= HALF else 0.0


def window_table(fine_axis):
    shape = (FINE, LANES) if fine_axis == 0 else (LANES, FINE)
    fine = lax.broadcasted_iota(jnp.int32, shape, fine_axis).astype(F32)
    coarse = lax.broadcasted_iota(jnp.int32, shape, 1 - fine_axis).astype(F32) - MARGIN
    distance = fine + 0.5 - RATIO * coarse - RATIO / 2
    table = jnp.maximum(0.0, 1.0 - jnp.abs(distance) / RATIO).astype(BF16)
    return jnp.concatenate([table, table], axis=0)


class Sizes:
    def __init__(self, mesh, perturbations, control):
        self.n_mem = mesh.shape["mem"]
        self.n_lat = mesh.shape["lat"]
        self.members = control.shape[0]
        self.group = self.members // GROUPS
        self.rows = control.shape[1]
        self.cols = control.shape[2]
        self.vars = perturbations.shape[1]
        self.fine_rows = perturbations.shape[2]
        self.fine_cols = perturbations.shape[3]
        assert self.rows == REACH and self.cols % LANES == WIN
        assert self.fine_rows == RATIO * self.rows and self.fine_cols == RATIO * self.cols
        self.windows = self.cols // WIN
        self.ext = self.cols + 2 * MARGIN
        self.slab = self.rows * self.group
        self.full = self.cols // LANES
        self.packed = self.full * self.slab + self.slab // 2
        self.field_rows = self.vars * self.fine_rows
        self.share = self.fine_cols // self.n_mem
        self.share_full = self.share // LANES
        self.share_rem = self.share % LANES
        self.groups = LANES // self.share_rem if self.share_rem else 1
        self.rem_rows = -(-self.field_rows // 8 // self.groups) * 8 if self.share_rem else 0
        self.share_rows = self.share_full * self.field_rows + self.rem_rows
        self.field_tiles = self.fine_cols // LANES
        self.part_rows = -(-self.field_tiles * self.field_rows // 8 // self.n_mem) * 8
        self.list_rows = self.part_rows * self.n_mem


def lane(shape):
    return lax.broadcasted_iota(jnp.int32, shape, 1)


def half_turn(x):
    return pltpu.roll(x, WIN, 1)


def pack_slab(size, first, last, middle):
    rows = size.slab
    at = lane((rows, LANES))
    pieces = list(middle)
    pieces.append(jnp.where(at < LANES - MARGIN, last, first))
    half = rows // 2
    at = lane((half, LANES))
    inner = (at >= MARGIN) & (at < LANES - MARGIN)
    pieces.append(jnp.where(inner, first[:half], half_turn(first[half:])))
    return pieces


def unpack_slab(size, packed):
    rows = size.slab
    middle = [packed[i * rows : (i + 1) * rows] for i in range(size.full - 1)]
    mixed = packed[(size.full - 1) * rows : size.full * rows]
    rest = packed[size.full * rows :]
    rest = jnp.concatenate([rest, half_turn(rest)], axis=0)
    at = lane((rows, LANES))
    first = jnp.where(at < MARGIN, half_turn(mixed), jnp.where(at < LANES - MARGIN, rest, mixed))
    last = jnp.where(at < LANES - MARGIN, mixed, half_turn(rest))
    return [first] + middle + [last]


def tiles_of(ref, count):
    return [ref[:, i * LANES : (i + 1) * LANES] for i in range(count)]


def put_packed(out, pieces):
    at = 0
    for piece in pieces:
        out[at : at + piece.shape[0], :] = piece
        at += piece.shape[0]


def pack_ref(size, out, tiles):
    put_packed(out, pack_slab(size, tiles[0], tiles[-1], tiles[1:-1]))


def place():
    lat = lax.axis_index("lat")
    odd = lax.rem(lat, 2) == 1
    low = (lat > 0).astype(F32)
    high = (lat < lax.axis_size("lat") - 1).astype(F32)
    return odd, low, high


def sides(a, b):
    odd, low, high = place()
    lower = jnp.where(odd, a, b) * low
    upper = jnp.where(odd, b, a) * high
    return lower, upper


def step_length(scal_ref):
    total = jnp.sum(scal_ref[...], axis=0, keepdims=True)
    at = lane(total.shape)
    grad_sq = jnp.sum(jnp.where(at == 0, total, 0.0), axis=1, keepdims=True)
    image_sq = jnp.sum(jnp.where(at == 1, total, 0.0), axis=1, keepdims=True)
    return grad_sq / (grad_sq + image_sq)


def enter_kernel(size, control_ref, *outs):
    for g in range(GROUPS):
        own_ref, packed_ref = outs[2 * g : 2 * g + 2]
        x = jnp.concatenate(
            [
                control_ref[pl.ds(r * size.members + g * size.group, size.group), :]
                for r in range(size.rows)
            ],
            axis=0,
        )
        own_ref[...] = jnp.concatenate([x[:, size.cols - MARGIN :], x, x[:, :MARGIN]], axis=1)
        pack_ref(size, packed_ref, tiles_of(own_ref, size.ext // LANES))


def load_kernel(pert_ref, out_ref, sems):
    count = sems.shape[0]
    part = pert_ref.shape[0] // count
    copies = [
        pltpu.make_async_copy(
            pert_ref.at[pl.ds(i * part, part)], out_ref.at[pl.ds(i * part, part)], sems.at[i]
        )
        for i in range(count)
    ]
    for copy in copies:
        copy.start()
    for copy in copies:
        copy.wait()


def forward_kernel(size, g, shares, own_ref, a_ref, b_ref, pert_ref, *rest):
    rest = list(rest)
    start_ref = rest.pop(0) if g else None
    last = g == GROUPS - 1
    outs = [rest.pop(0) for i in range(size.n_mem if last else 1)]
    ext_ref, coarse_ref, rows_ref = rest[:3]
    acc_ref = rest[3] if last else outs[0]
    members = size.group
    n_tiles = size.ext // LANES
    fine_rows = size.fine_rows

    unused, low, high = place()
    lower, upper = sides(a_ref[...], b_ref[...])
    lower = unpack_slab(size, lower)
    upper = unpack_slab(size, upper)
    n = size.slab
    for e in range(n_tiles):
        cut = slice(e * LANES, (e + 1) * LANES)
        ext_ref[0:n, cut] = lower[e]
        ext_ref[n : 2 * n, cut] = own_ref[:, cut]
        ext_ref[2 * n : 3 * n, cut] = upper[e]
    for e in range(n_tiles):
        cut = slice(e * LANES, (e + 1) * LANES)
        for at in range(0, members, 8):
            held = [
                ext_ref[k * members + at : k * members + at + 8, cut] for k in range(3 * REACH)
            ]
            for j in range(size.rows + 2):
                total = None
                for k in range(3 * REACH):
                    weight = smooth(j - 1 - (k - REACH))
                    if weight:
                        term = held[k] * weight
                        total = term if total is None else total + term
                if j == 0:
                    total = total * low
                if j == size.rows + 1:
                    total = total * high
                coarse_ref[j * members + at : j * members + at + 8, cut] = total
    for t in range(size.windows):
        e = t // 2
        held = []
        for j in range(size.rows + 2):
            at = slice(j * members, (j + 1) * members)
            value = coarse_ref[at, e * LANES : (e + 1) * LANES]
            if t % 2:
                other = coarse_ref[at, (e + 1) * LANES : (e + 2) * LANES]
                value = half_turn(jnp.where(lane(value.shape) < WIN, other, value))
            held.append(value)
        for i in range(fine_rows):
            total = None
            for j in range(size.rows + 2):
                weight = tent(i + 0.5 - RATIO * (j - 1) - RATIO / 2)
                if weight:
                    term = held[j] * weight
                    total = term if total is None else total + term
            rows_ref[t, pl.ds(i, members, stride=fine_rows), :] = total
    table = window_table(1)
    block = CHUNK * fine_rows

    def chunk(step, unused):
        first = pl.multiple_of(step * block, 8)
        for t in range(size.windows):
            x = rows_ref[t, pl.ds(first, block), :]
            head = x.astype(BF16)
            tail = (x - head.astype(F32)).astype(BF16)
            refined = jnp.dot(
                jnp.concatenate([head, tail], axis=1), table, preferred_element_type=F32
            )
            for e in range(t * FINE // LANES, (t + 1) * FINE // LANES):
                cut = slice(e * LANES, (e + 1) * LANES)
                here = slice(e * LANES - t * FINE, (e + 1) * LANES - t * FINE)
                rows = [
                    pl.ds(e * size.field_rows + v * fine_rows, fine_rows)
                    for v in range(size.vars)
                ]
                totals = [acc_ref[at, :] for at in rows]
                for m in range(CHUNK):
                    value = refined[m * fine_rows : (m + 1) * fine_rows, here]
                    for v in range(size.vars):
                        pert = pert_ref[g * members + step * CHUNK + m, v, :, cut].astype(F32)
                        totals[v] = totals[v] + pert * value
                for v in range(size.vars):
                    acc_ref[rows[v], :] = totals[v]
        return unused

    if g:
        acc_ref[...] = start_ref[...]
    else:
        acc_ref[...] = jnp.zeros_like(acc_ref)
    lax.fori_loop(0, members // CHUNK, chunk, 0)
    if not last:
        return
    mine = lax.axis_index("mem")
    if shares:
        parts_ref = rest[4]
        for q in range(size.n_mem):
            put_share(size, parts_ref.at[q], acc_ref, q * size.share)
        for d in range(size.n_mem):
            outs[d][...] = parts_ref[mine ^ d]
    else:
        for d in range(size.n_mem):
            first = pl.multiple_of((mine ^ d) * size.part_rows, 8)
            outs[d][...] = acc_ref[pl.ds(first, size.part_rows), :]


def field_tile(size, list_ref, start):
    e, shift = start // LANES, start % LANES
    rows = size.field_rows
    tile = list_ref[e * rows : (e + 1) * rows, :]
    if shift == 0:
        return tile
    if e + 1 < size.field_tiles:
        other = list_ref[(e + 1) * rows : (e + 2) * rows, :]
        tile = jnp.where(lane(tile.shape) < shift, other, tile)
    return pltpu.roll(tile, LANES - shift, 1)


def put_share(size, out, list_ref, start):
    rows = size.field_rows
    for j in range(size.share_full):
        out[j * rows : (j + 1) * rows, :] = field_tile(size, list_ref, start + j * LANES)
    if size.share_rem:
        tile = field_tile(size, list_ref, start + size.share_full * LANES)
        tile = jnp.where(lane(tile.shape) < size.share_rem, tile, 0.0)
        missing = size.rem_rows * size.groups - rows
        if missing:
            tile = jnp.concatenate([tile, jnp.zeros((missing, LANES), F32)], axis=0)
        total = None
        for g in range(size.groups):
            term = tile[g * size.rem_rows : (g + 1) * size.rem_rows]
            if g:
                term = pltpu.roll(term, g * size.share_rem, 1)
            total = term if total is None else total + term
        out[size.share_full * rows :, :] = total


def share_tiles(size, part):
    rows = size.field_rows
    tiles = [(part[j * rows : (j + 1) * rows], LANES) for j in range(size.share_full)]
    if size.share_rem:
        rest = part[size.share_full * rows :]
        stack = [rest]
        for g in range(1, size.groups):
            stack.append(pltpu.roll(rest, LANES - g * size.share_rem, 1))
        tiles.append((jnp.concatenate(stack, axis=0)[:rows], size.share_rem))
    return tiles


def total_kernel(count, *refs):
    parts, out_ref = refs[:count], refs[count]
    total = parts[0][...]
    for part in parts[1:]:
        total = total + part[...]
    out_ref[...] = total


def squares_kernel(count, *refs):
    parts, grads = refs[:count], refs[count : count + GROUPS]
    out_ref, scal_ref = refs[count + GROUPS :]
    total = parts[0][...]
    for part in parts[1:]:
        total = total + part[...]
    out_ref[...] = total
    image_sq = jnp.sum(total * total)
    grad_sq = sum(jnp.sum(grad[...] * grad[...]) for grad in grads)
    at = lane(scal_ref.shape)
    scal_ref[...] = jnp.where(at == 0, grad_sq, jnp.where(at == 1, image_sq, 0.0))


def misfit_of(size, parts, before_ref, scal_ref, innov_ref, limit_ref, list_ref, misfit_ref):
    fine_rows = size.fine_rows
    mine = lax.axis_index("mem")
    for d in range(size.n_mem):
        first = pl.multiple_of((mine ^ d) * size.part_rows, 8)
        list_ref[pl.ds(first, size.part_rows), :] = parts[d][...]
    if before_ref is not None:
        length = step_length(scal_ref)
    for e in range(size.field_tiles):
        cut = slice(e * LANES, (e + 1) * LANES)
        for v in range(size.vars):
            at = pl.ds(e * size.field_rows + v * fine_rows, fine_rows)
            value = list_ref[at, :]
            if before_ref is not None:
                value = before_ref[at, :] - length * value
            limit = limit_ref[:, v : v + 1]
            misfit_ref[at, :] = jnp.clip(value - innov_ref[v, :, cut], -limit, limit)


def adjoint_kernel(size, g, later, *refs):
    refs = list(refs)
    pert_ref = refs.pop(0)
    if g == 0:
        parts = [refs.pop(0) for i in range(size.n_mem)]
        scal_ref, before_ref = (refs.pop(0), refs.pop(0)) if later else (None, None)
        innov_ref, limit_ref = refs.pop(0), refs.pop(0)
    else:
        misfit_ref = refs.pop(0)
    a_ref, b_ref, own_ref = refs[:3]
    refs = refs[3:]
    if g == 0:
        misfit_ref = refs.pop(0)
        list_ref = refs.pop(0)
    cols_ref, coarse_ref, spread_ref = refs[:3]
    members = size.group
    n_tiles = size.ext // LANES
    fine_rows = size.fine_rows
    if g == 0:
        misfit_of(size, parts, before_ref, scal_ref, innov_ref, limit_ref, list_ref, misfit_ref)
    table = window_table(0)
    block = CHUNK * fine_rows

    def chunk(step, unused):
        first = pl.multiple_of(step * block, 8)
        tops = [None] * n_tiles
        for t in range(size.windows):
            cut = slice(t * FINE, (t + 1) * FINE)
            tiles = range(t * FINE // LANES, (t + 1) * FINE // LANES)
            mis = [
                jnp.concatenate(
                    [
                        misfit_ref[pl.ds(e * size.field_rows + v * fine_rows, fine_rows), :]
                        for e in tiles
                    ],
                    axis=1,
                )
                for v in range(size.vars)
            ]
            weighted = []
            for m in range(CHUNK):
                total = pert_ref[g * members + step * CHUNK + m, 0, :, cut].astype(F32) * mis[0]
                for v in range(1, size.vars):
                    total = total + pert_ref[g * members + step * CHUNK + m, v, :, cut].astype(F32) * mis[v]
                weighted.append(total)
            x = jnp.concatenate(weighted, axis=0)
            head = x.astype(BF16)
            tail = (x - head.astype(F32)).astype(BF16)
            columns = jnp.dot(
                jnp.concatenate([head, tail], axis=1), table, preferred_element_type=F32
            )
            e = t // 2
            if t % 2 == 0:
                tops[e] = columns if tops[e] is None else tops[e] + columns
            else:
                turned = half_turn(columns)
                at = lane(turned.shape)
                tops[e] = tops[e] + jnp.where(at >= WIN, turned, 0.0)
                tops[e + 1] = jnp.where(at < WIN, turned, 0.0)
        for e in range(n_tiles):
            cols_ref[e, pl.ds(first, block), :] = tops[e]
        return unused

    lax.fori_loop(0, members // CHUNK, chunk, 0)
    odd, low, high = place()
    for e in range(n_tiles):
        cut = slice(e * LANES, (e + 1) * LANES)
        sums = [None] * (size.rows + 2)
        for i in range(fine_rows):
            value = cols_ref[e, pl.ds(i, members, stride=fine_rows), :]
            for j in range(size.rows + 2):
                weight = tent(i + 0.5 - RATIO * (j - 1) - RATIO / 2)
                if weight:
                    term = value * weight
                    sums[j] = term if sums[j] is None else sums[j] + term
        sums[0] = sums[0] * low
        sums[-1] = sums[-1] * high
        for j in range(size.rows + 2):
            coarse_ref[j * members : (j + 1) * members, cut] = sums[j]
    head = coarse_ref[:, 0:LANES]
    tail = coarse_ref[:, (n_tiles - 1) * LANES :]
    at = lane(head.shape)
    turned_head, turned_tail = half_turn(head), half_turn(tail)
    coarse_ref[:, 0:LANES] = head + jnp.where(at < WIN, turned_tail, 0.0)
    coarse_ref[:, (n_tiles - 1) * LANES :] = tail + jnp.where(at >= WIN, turned_head, 0.0)
    for e in range(n_tiles):
        cut = slice(e * LANES, (e + 1) * LANES)
        for at in range(0, members, 8):
            held = [
                coarse_ref[j * members + at : j * members + at + 8, cut]
                for j in range(size.rows + 2)
            ]
            for k in range(3 * REACH):
                total = None
                for j in range(size.rows + 2):
                    weight = smooth(j - 1 - (k - REACH))
                    if weight:
                        term = held[j] * weight
                        total = term if total is None else total + term
                spread_ref[k * members + at : k * members + at + 8, cut] = total
    n = size.slab

    def packed_of(part):
        tiles = [
            spread_ref[part * n : (part + 1) * n, e * LANES : (e + 1) * LANES]
            for e in range(n_tiles)
        ]
        return pack_slab(size, tiles[0], tiles[-1], tiles[1:-1])

    lower, upper = packed_of(0), packed_of(2)
    own_ref[...] = spread_ref[n : 2 * n, :]
    put_packed(a_ref, [jnp.where(odd, x, y) for x, y in zip(lower, upper)])
    put_packed(b_ref, [jnp.where(odd, y, x) for x, y in zip(lower, upper)])


def gradient_kernel(size, later, *refs):
    refs = list(refs)
    own_ref, a_ref, b_ref, weights_ref = refs[:4]
    refs = refs[4:]
    weights = weights_ref[...]
    if later:
        scal_ref, before_ref = refs.pop(0), refs.pop(0)
        weights = weights - step_length(scal_ref) * before_ref[...]
    grad_ref, packed_ref = refs[:2]
    if later:
        refs[2][...] = weights
    lower, upper = sides(a_ref[...], b_ref[...])
    arrived = unpack_slab(size, lower + upper)
    for e in range(size.ext // LANES):
        cut = slice(e * LANES, (e + 1) * LANES)
        grad_ref[:, cut] = weights[:, cut] + own_ref[:, cut] + arrived[e]
    pack_ref(size, packed_ref, tiles_of(grad_ref, size.ext // LANES))


def own_share_kernel(size, before_ref, image_ref, scal_ref, out_ref, list_ref, shares_ref):
    list_ref[...] = before_ref[...] - step_length(scal_ref) * image_ref[...]
    for q in range(size.n_mem):
        put_share(size, shares_ref.at[q], list_ref, q * size.share)
    out_ref[...] = shares_ref[lax.axis_index("mem")]


def leave_kernel(size, *refs):
    weights_refs, grad_refs = refs[:GROUPS], refs[GROUPS : 2 * GROUPS]
    field_ref, image_ref, scal1_ref = refs[2 * GROUPS : 2 * GROUPS + 3]
    out_weights_ref, out_field_ref = refs[2 * GROUPS + 3 :]
    second = step_length(scal1_ref)
    n_tiles = size.ext // LANES
    for g in range(GROUPS):
        weights = weights_refs[g][...] - second * grad_refs[g][...]
        tiles = [weights[:, e * LANES : (e + 1) * LANES] for e in range(n_tiles)]
        for e in range(n_tiles):
            tile = tiles[e]
            if e + 1 < n_tiles:
                tile = jnp.where(lane(tile.shape) < MARGIN, tiles[e + 1], tile)
            tile = pltpu.roll(tile, LANES - MARGIN, 1)
            start = e * LANES
            width = min(LANES, size.cols - start)
            for r in range(size.rows):
                to = pl.ds(r * size.members + g * size.group, size.group)
                rows = slice(r * size.group, (r + 1) * size.group)
                out_weights_ref[to, start : start + width] = tile[rows, :width]
    field = field_ref[...] - second * image_ref[...]
    start = 0
    for tile, width in share_tiles(size, field):
        for v in range(size.vars):
            rows = slice(v * size.fine_rows, (v + 1) * size.fine_rows)
            out_field_ref[v, :, start : start + width] = tile[rows, :width]
        start += width


def whole():
    return pl.BlockSpec(memory_space=pltpu.VMEM)


def params():
    return pltpu.CompilerParams(vmem_limit_bytes=24 * 1024 * 1024)


def array(*shape):
    return jax.ShapeDtypeStruct(shape, F32)


def call(kernel, outs, *args, scratch=(), flops=0, spaces=None):
    spaces = spaces or [
        pltpu.MemorySpace.SMEM if arg.ndim == 1 else pltpu.MemorySpace.VMEM for arg in args
    ]
    moved = sum(arg.size * arg.dtype.itemsize for arg in args)
    return pl.pallas_call(
        kernel,
        out_shape=outs,
        in_specs=[pl.BlockSpec(memory_space=space) for space in spaces],
        out_specs=jax.tree.map(lambda unused: whole(), outs),
        scratch_shapes=scratch,
        compiler_params=params(),
        cost_estimate=pl.CostEstimate(flops=flops, bytes_accessed=moved, transcendentals=0),
    )(*args)


def per_device(mesh, perturbations, control, innovations, thresholds):
    size = Sizes(mesh, perturbations, control)
    n_mem, n_lat, members = size.n_mem, size.n_lat, size.members
    devices = n_mem * n_lat
    pairs = [(i, i ^ 1) for i in range(n_lat)]
    cross = [(i, (i - 1 if i % 2 == 0 else i + 1) % n_lat) for i in range(n_lat)]
    far_first = sorted(range(1, n_mem), key=lambda d: -d)
    groups = range(GROUPS)
    slab = array(size.slab, size.ext)
    packed = array(size.packed, LANES)
    part = array(size.part_rows, LANES)
    share = array(size.share_rows, LANES)
    scal = array(devices, LANES)
    field = array(size.list_rows, LANES)
    map_flops = 4 * size.group * size.fine_rows * size.fine_cols * 2 * LANES

    def swap(to_a, to_b):
        return lax.ppermute(to_a, "lat", pairs), lax.ppermute(to_b, "lat", cross)

    def exchange(parts):
        moved = {
            d: lax.ppermute(parts[d], "mem", [(i, i ^ d) for i in range(n_mem)])
            for d in far_first
        }
        return [parts[0]] + [moved[d] for d in range(1, n_mem)]

    def forward(owns, arrived, shares=False):
        acc = []
        piece = share if shares else part
        for g in groups:
            last = g == GROUPS - 1
            scratch = [
                pltpu.VMEM((3 * size.slab, size.ext), F32),
                pltpu.VMEM(((size.rows + 2) * size.group, size.ext), F32),
                pltpu.VMEM((size.windows, size.group * size.fine_rows, LANES), F32),
            ]
            if last:
                scratch.append(pltpu.VMEM(field.shape, F32))
                if shares:
                    scratch.append(pltpu.VMEM((n_mem, *piece.shape), F32))
            acc = call(
                functools.partial(forward_kernel, size, g, shares),
                [piece] * n_mem if last else [field],
                owns[g],
                *arrived[g],
                resident,
                *acc,
                scratch=scratch,
                flops=map_flops,
            )
        return exchange(acc)

    def adjoint(parts, *step):
        later = len(step) > 0
        sent, spread, misfit, whole_field = [], [], None, None
        for g in groups:
            scratch = [
                pltpu.VMEM((size.ext // LANES, size.group * size.fine_rows, LANES), F32),
                pltpu.VMEM(((size.rows + 2) * size.group, size.ext), F32),
                pltpu.VMEM((3 * size.slab, size.ext), F32),
            ]
            outs = [packed, packed, slab]
            args = [misfit]
            if g == 0:
                outs += [field, field]
                args = [*parts, *step, innovations, thresholds.reshape(1, size.vars)]
            results = call(
                functools.partial(adjoint_kernel, size, g, later),
                outs,
                resident,
                *args,
                scratch=scratch,
                flops=map_flops,
            )
            sent.append(swap(*results[:2]))
            spread.append(results[2])
            if g == 0:
                misfit = results[3]
                whole_field = results[4]
        return sent, spread, whole_field

    def gradient(arrived, spread, weights, *step):
        later = len(step) > 0
        grads, sent, olds = [], [], []
        for g in groups:
            results = call(
                functools.partial(gradient_kernel, size, later),
                [slab, packed] + ([slab] if later else []),
                spread[g],
                *arrived[g],
                weights[g],
                *([step[0], step[1][g]] if later else []),
            )
            grads.append(results[0])
            sent.append(results[1])
            olds.append(results[2] if later else weights[g])
        return grads, sent, olds

    def squares(parts, sent):
        return call(
            functools.partial(squares_kernel, n_mem),
            [array(*parts[0].shape), scal],
            *parts,
            *sent,
        )

    def everywhere(tile):
        moved = lax.all_to_all(tile.reshape(devices, 1, LANES), ("mem", "lat"), 0, 0)
        return moved.reshape(devices, LANES)

    def both(sent):
        return [swap(x, x) for x in sent]

    entered = call(
        functools.partial(enter_kernel, size),
        [slab, packed] * GROUPS,
        control.transpose(1, 0, 2).reshape(size.rows * members, size.cols),
    )
    control_own, sent = entered[0::2], entered[1::2]
    copies = min(4, members)
    resident = call(
        load_kernel,
        jax.ShapeDtypeStruct(perturbations.shape, perturbations.dtype),
        perturbations,
        scratch=[pltpu.SemaphoreType.DMA((copies,))],
        spaces=[pltpu.MemorySpace.HBM],
        flops=2 * map_flops,
    )
    parts = forward(control_own, both(sent))
    field0 = call(functools.partial(total_kernel, n_mem), part, *parts)
    arrived, spread, before = adjoint(exchange([field0] * n_mem))
    grads0, sent, unused = gradient(arrived, spread, control_own)
    parts = forward(grads0, both(sent))
    image0, scal0 = squares(parts, sent)
    images = exchange([image0] * n_mem)
    scal0 = everywhere(scal0)
    arrived, spread, image_all = adjoint(images, scal0, before)
    grads1, sent, weights1 = gradient(arrived, spread, control_own, scal0, grads0)
    own_share = call(
        functools.partial(own_share_kernel, size),
        share,
        before,
        image_all,
        scal0,
        scratch=[pltpu.VMEM(field.shape, F32), pltpu.VMEM((n_mem, *share.shape), F32)],
        flops=map_flops // 8,
    )
    parts = forward(grads1, both(sent), shares=True)
    image1, scal1 = squares(parts, sent)
    scal1 = everywhere(scal1)
    weights, result = call(
        functools.partial(leave_kernel, size),
        [
            array(size.rows * members, size.cols),
            array(size.vars, size.fine_rows, size.share),
        ],
        *weights1,
        *grads1,
        own_share,
        image1,
        scal1,
    )
    return weights.reshape(size.rows, members, size.cols).transpose(1, 0, 2), result


def solution(mesh):
    return jax.shard_map(
        functools.partial(per_device, mesh),
        mesh=mesh,
        in_specs=(P("mem", None, "lat", None), P("mem", "lat", None), P(None, "lat", None), P()),
        out_specs=(P("mem", "lat", None), P(None, "lat", "mem")),
        check_vma=False,
    )
```

```python
import functools

import jax
import jax.numpy as jnp
from jax import lax
from jax.experimental import pallas as pl
from jax.experimental.pallas import tpu as pltpu
from jax.sharding import PartitionSpec as P

RATIO = 4
HALF = 5
STEPS = 2
REACH = HALF + 1
LANES = 128
WIN = 64
MARGIN = 32
FINE = RATIO * WIN
CHUNK = 16
GROUPS = 2
F32 = jnp.float32
BF16 = jnp.bfloat16


def tent(distance):
    return max(0.0, 1.0 - abs(distance) / RATIO)


def smooth(distance):
    return (1.0 - abs(distance) / REACH) / 2 if abs(distance) <= HALF else 0.0


def window_table(fine_axis):
    shape = (FINE, LANES) if fine_axis == 0 else (LANES, FINE)
    fine = lax.broadcasted_iota(jnp.int32, shape, fine_axis).astype(F32)
    coarse = lax.broadcasted_iota(jnp.int32, shape, 1 - fine_axis).astype(F32) - MARGIN
    distance = fine + 0.5 - RATIO * coarse - RATIO / 2
    table = jnp.maximum(0.0, 1.0 - jnp.abs(distance) / RATIO).astype(BF16)
    return jnp.concatenate([table, table], axis=0)


class Sizes:
    def __init__(self, mesh, perturbations, control):
        self.n_mem = mesh.shape["mem"]
        self.n_lat = mesh.shape["lat"]
        self.far_first = range(self.n_mem - 1, 0, -1)
        self.members = control.shape[0]
        self.group = self.members // GROUPS
        self.rows = control.shape[1]
        self.cols = control.shape[2]
        self.vars = perturbations.shape[1]
        self.fine_rows = perturbations.shape[2]
        self.fine_cols = perturbations.shape[3]
        assert self.rows == REACH and self.cols % LANES == WIN
        assert self.fine_rows == RATIO * self.rows and self.fine_cols == RATIO * self.cols
        self.windows = self.cols // WIN
        self.ext = self.cols + 2 * MARGIN
        self.slab = self.rows * self.group
        self.full = self.cols // LANES
        self.packed = self.full * self.slab + self.slab // 2
        self.field_rows = self.vars * self.fine_rows
        self.share = self.fine_cols // self.n_mem
        self.share_full = self.share // LANES
        self.share_rem = self.share % LANES
        self.groups = LANES // self.share_rem if self.share_rem else 1
        self.rem_rows = -(-self.field_rows // 8 // self.groups) * 8 if self.share_rem else 0
        self.share_rows = self.share_full * self.field_rows + self.rem_rows
        self.field_tiles = self.fine_cols // LANES
        self.part_rows = -(-self.field_tiles * self.field_rows // 8 // self.n_mem) * 8
        self.list_rows = self.part_rows * self.n_mem


def lane(shape):
    return lax.broadcasted_iota(jnp.int32, shape, 1)


def half_turn(x):
    return pltpu.roll(x, WIN, 1)


def pack_slab(size, first, last, middle):
    rows = size.slab
    at = lane((rows, LANES))
    pieces = list(middle)
    pieces.append(jnp.where(at < LANES - MARGIN, last, first))
    half = rows // 2
    at = lane((half, LANES))
    inner = (at >= MARGIN) & (at < LANES - MARGIN)
    pieces.append(jnp.where(inner, first[:half], half_turn(first[half:])))
    return pieces


def unpack_slab(size, packed):
    rows = size.slab
    middle = [packed[i * rows : (i + 1) * rows] for i in range(size.full - 1)]
    mixed = packed[(size.full - 1) * rows : size.full * rows]
    rest = packed[size.full * rows :]
    rest = jnp.concatenate([rest, half_turn(rest)], axis=0)
    at = lane((rows, LANES))
    first = jnp.where(at < MARGIN, half_turn(mixed), jnp.where(at < LANES - MARGIN, rest, mixed))
    last = jnp.where(at < LANES - MARGIN, mixed, half_turn(rest))
    return [first] + middle + [last]


def tiles_of(ref, count):
    return [ref[:, i * LANES : (i + 1) * LANES] for i in range(count)]


def put_packed(out, pieces):
    at = 0
    for piece in pieces:
        out[at : at + piece.shape[0], :] = piece
        at += piece.shape[0]


def pack_ref(size, out, tiles):
    put_packed(out, pack_slab(size, tiles[0], tiles[-1], tiles[1:-1]))


def place():
    lat = lax.axis_index("lat")
    odd = lax.rem(lat, 2) == 1
    low = (lat > 0).astype(F32)
    high = (lat < lax.axis_size("lat") - 1).astype(F32)
    return odd, low, high


def sides(a, b):
    odd, low, high = place()
    lower = jnp.where(odd, a, b) * low
    upper = jnp.where(odd, b, a) * high
    return lower, upper


def step_length(scal_ref):
    total = jnp.sum(scal_ref[...], axis=0, keepdims=True)
    at = lane(total.shape)
    grad_sq = jnp.sum(jnp.where(at == 0, total, 0.0), axis=1, keepdims=True)
    image_sq = jnp.sum(jnp.where(at == 1, total, 0.0), axis=1, keepdims=True)
    return grad_sq / (grad_sq + image_sq)


def enter_kernel(size, control_ref, *outs):
    for g in range(GROUPS):
        own_ref, packed_ref = outs[2 * g : 2 * g + 2]
        x = jnp.concatenate(
            [
                control_ref[pl.ds(r * size.members + g * size.group, size.group), :]
                for r in range(size.rows)
            ],
            axis=0,
        )
        own_ref[...] = jnp.concatenate([x[:, size.cols - MARGIN :], x, x[:, :MARGIN]], axis=1)
        pack_ref(size, packed_ref, tiles_of(own_ref, size.ext // LANES))


def load_kernel(pert_ref, out_ref, held_ref, sems):
    count = sems.shape[0]
    part = pert_ref.shape[0] // count
    copies = [
        pltpu.make_async_copy(
            pert_ref.at[pl.ds(i * part, part)], held_ref.at[pl.ds(i * part, part)], sems.at[i]
        )
        for i in range(count)
    ]
    for copy in copies:
        copy.start()
    for i, copy in enumerate(copies):
        copy.wait()

        def widen(m, unused):
            for v in range(pert_ref.shape[1]):
                out_ref[m, v] = held_ref[m, v].astype(F32)
            return unused

        lax.fori_loop(i * part, (i + 1) * part, widen, 0)


def forward_kernel(size, g, shares, own_ref, b_ref, a_ref, pert_ref, *rest):
    rest = list(rest)
    start_ref = rest.pop(0) if g else None
    last = g == GROUPS - 1
    extra = shares and g == 0
    if extra:
        sources = [rest.pop(0) for i in range(3)]
    outs = [rest.pop(0) for i in range(size.n_mem if last else 1)]
    if extra:
        own_share_kernel(size, *sources, rest.pop(0), *rest[-2:])
    ext_ref, coarse_ref, rows_ref = rest[:3]
    acc_ref = rest[3] if last else outs[0]
    members = size.group
    n_tiles = size.ext // LANES
    fine_rows = size.fine_rows

    unused, low, high = place()
    lower, upper = sides(a_ref[...], b_ref[...])
    lower = unpack_slab(size, lower)
    upper = unpack_slab(size, upper)
    n = size.slab
    for e in range(n_tiles):
        cut = slice(e * LANES, (e + 1) * LANES)
        ext_ref[0:n, cut] = lower[e]
        ext_ref[n : 2 * n, cut] = own_ref[:, cut]
        ext_ref[2 * n : 3 * n, cut] = upper[e]
    for e in range(n_tiles):
        cut = slice(e * LANES, (e + 1) * LANES)
        for at in range(0, members, 8):
            held = [
                ext_ref[k * members + at : k * members + at + 8, cut] for k in range(3 * REACH)
            ]
            for j in range(size.rows + 2):
                total = None
                for k in range(3 * REACH):
                    weight = smooth(j - 1 - (k - REACH))
                    if weight:
                        term = held[k] * weight
                        total = term if total is None else total + term
                if j == 0:
                    total = total * low
                if j == size.rows + 1:
                    total = total * high
                coarse_ref[j * members + at : j * members + at + 8, cut] = total
    for t in range(size.windows):
        e = t // 2
        held = []
        for j in range(size.rows + 2):
            at = slice(j * members, (j + 1) * members)
            value = coarse_ref[at, e * LANES : (e + 1) * LANES]
            if t % 2:
                other = coarse_ref[at, (e + 1) * LANES : (e + 2) * LANES]
                value = half_turn(jnp.where(lane(value.shape) < WIN, other, value))
            held.append(value)
        for i in range(fine_rows):
            total = None
            for j in range(size.rows + 2):
                weight = tent(i + 0.5 - RATIO * (j - 1) - RATIO / 2)
                if weight:
                    term = held[j] * weight
                    total = term if total is None else total + term
            rows_ref[t, pl.ds(i, members, stride=fine_rows), :] = total
    table = window_table(1)
    block = CHUNK * fine_rows

    def chunk(step, unused):
        first = pl.multiple_of(step * block, 8)
        for t in range(size.windows):
            x = rows_ref[t, pl.ds(first, block), :]
            head = x.astype(BF16)
            tail = (x - head.astype(F32)).astype(BF16)
            refined = jnp.dot(
                jnp.concatenate([head, tail], axis=1), table, preferred_element_type=F32
            )
            for e in range(t * FINE // LANES, (t + 1) * FINE // LANES):
                cut = slice(e * LANES, (e + 1) * LANES)
                here = slice(e * LANES - t * FINE, (e + 1) * LANES - t * FINE)
                rows = [
                    pl.ds(e * size.field_rows + v * fine_rows, fine_rows)
                    for v in range(size.vars)
                ]
                totals = [acc_ref[at, :] for at in rows]
                for m in range(CHUNK):
                    value = refined[m * fine_rows : (m + 1) * fine_rows, here]
                    for v in range(size.vars):
                        pert = pert_ref[g * members + step * CHUNK + m, v, :, cut]
                        totals[v] = totals[v] + pert * value
                for v in range(size.vars):
                    acc_ref[rows[v], :] = totals[v]
        return unused

    if g:
        acc_ref[...] = start_ref[...]
    else:
        acc_ref[...] = jnp.zeros_like(acc_ref)
    lax.fori_loop(0, members // CHUNK, chunk, 0)
    if not last:
        return
    mine = lax.axis_index("mem")
    if shares:
        parts_ref = rest[4]
        for q in range(size.n_mem):
            put_share(size, parts_ref.at[q], acc_ref, q * size.share)
        for d in range(size.n_mem):
            outs[d][...] = parts_ref[mine ^ d]
    else:
        for d in range(size.n_mem):
            first = pl.multiple_of((mine ^ d) * size.part_rows, 8)
            outs[d][...] = acc_ref[pl.ds(first, size.part_rows), :]


def field_tile(size, list_ref, start):
    e, shift = start // LANES, start % LANES
    rows = size.field_rows
    tile = list_ref[e * rows : (e + 1) * rows, :]
    if shift == 0:
        return tile
    if e + 1 < size.field_tiles:
        other = list_ref[(e + 1) * rows : (e + 2) * rows, :]
        tile = jnp.where(lane(tile.shape) < shift, other, tile)
    return pltpu.roll(tile, LANES - shift, 1)


def put_share(size, out, list_ref, start):
    rows = size.field_rows
    for j in range(size.share_full):
        out[j * rows : (j + 1) * rows, :] = field_tile(size, list_ref, start + j * LANES)
    if size.share_rem:
        tile = field_tile(size, list_ref, start + size.share_full * LANES)
        tile = jnp.where(lane(tile.shape) < size.share_rem, tile, 0.0)
        missing = size.rem_rows * size.groups - rows
        if missing:
            tile = jnp.concatenate([tile, jnp.zeros((missing, LANES), F32)], axis=0)
        total = None
        for g in range(size.groups):
            term = tile[g * size.rem_rows : (g + 1) * size.rem_rows]
            if g:
                term = pltpu.roll(term, g * size.share_rem, 1)
            total = term if total is None else total + term
        out[size.share_full * rows :, :] = total


def share_tiles(size, part):
    rows = size.field_rows
    tiles = [(part[j * rows : (j + 1) * rows], LANES) for j in range(size.share_full)]
    if size.share_rem:
        rest = part[size.share_full * rows :]
        stack = [rest]
        for g in range(1, size.groups):
            stack.append(pltpu.roll(rest, LANES - g * size.share_rem, 1))
        tiles.append((jnp.concatenate(stack, axis=0)[:rows], size.share_rem))
    return tiles


def total_kernel(count, *refs):
    parts, out_ref = refs[:count], refs[count]
    total = parts[0][...]
    for part in parts[1:]:
        total = total + part[...]
    out_ref[...] = total


def squares_kernel(count, *refs):
    parts, grads = refs[:count], refs[count : count + GROUPS]
    out_ref, scal_ref = refs[count + GROUPS :]
    total = parts[0][...]
    for part in parts[1:]:
        total = total + part[...]
    out_ref[...] = total
    image_sq = jnp.sum(total * total)
    grad_sq = sum(jnp.sum(grad[...] * grad[...]) for grad in grads)
    at = lane(scal_ref.shape)
    scal_ref[...] = jnp.where(at == 0, grad_sq, jnp.where(at == 1, image_sq, 0.0))


def misfit_of(size, parts, before_ref, scal_ref, innov_ref, limit_ref, list_ref, misfit_ref):
    fine_rows = size.fine_rows
    mine = lax.axis_index("mem")
    for i, d in enumerate((0, *size.far_first)):
        first = pl.multiple_of((mine ^ d) * size.part_rows, 8)
        list_ref[pl.ds(first, size.part_rows), :] = parts[i][...]
    if before_ref is not None:
        length = step_length(scal_ref)
    for e in range(size.field_tiles):
        cut = slice(e * LANES, (e + 1) * LANES)
        for v in range(size.vars):
            at = pl.ds(e * size.field_rows + v * fine_rows, fine_rows)
            value = list_ref[at, :]
            if before_ref is not None:
                value = before_ref[at, :] - length * value
            limit = limit_ref[:, v : v + 1]
            misfit_ref[at, :] = jnp.clip(value - innov_ref[v, :, cut], -limit, limit)


def adjoint_kernel(size, g, later, *refs):
    refs = list(refs)
    pert_ref = refs.pop(0)
    if g == 0:
        parts = [refs.pop(0) for i in range(size.n_mem)]
        scal_ref, before_ref = (refs.pop(0), refs.pop(0)) if later else (None, None)
        innov_ref, limit_ref = refs.pop(0), refs.pop(0)
    else:
        misfit_ref = refs.pop(0)
    a_ref, b_ref, own_ref = refs[:3]
    refs = refs[3:]
    if g == 0:
        misfit_ref = refs.pop(0)
        list_ref = refs.pop(0)
    cols_ref, coarse_ref, spread_ref = refs[:3]
    members = size.group
    n_tiles = size.ext // LANES
    fine_rows = size.fine_rows
    if g == 0:
        misfit_of(size, parts, before_ref, scal_ref, innov_ref, limit_ref, list_ref, misfit_ref)
    table = window_table(0)
    block = CHUNK * fine_rows

    def chunk(step, unused):
        first = pl.multiple_of(step * block, 8)
        tops = [None] * n_tiles
        for t in range(size.windows):
            cut = slice(t * FINE, (t + 1) * FINE)
            tiles = range(t * FINE // LANES, (t + 1) * FINE // LANES)
            mis = [
                jnp.concatenate(
                    [
                        misfit_ref[pl.ds(e * size.field_rows + v * fine_rows, fine_rows), :]
                        for e in tiles
                    ],
                    axis=1,
                )
                for v in range(size.vars)
            ]
            weighted = []
            for m in range(CHUNK):
                total = pert_ref[g * members + step * CHUNK + m, 0, :, cut]* mis[0]
                for v in range(1, size.vars):
                    total = total + pert_ref[g * members + step * CHUNK + m, v, :, cut]* mis[v]
                weighted.append(total)
            x = jnp.concatenate(weighted, axis=0)
            head = x.astype(BF16)
            tail = (x - head.astype(F32)).astype(BF16)
            columns = jnp.dot(
                jnp.concatenate([head, tail], axis=1), table, preferred_element_type=F32
            )
            e = t // 2
            if t % 2 == 0:
                tops[e] = columns if tops[e] is None else tops[e] + columns
            else:
                turned = half_turn(columns)
                at = lane(turned.shape)
                tops[e] = tops[e] + jnp.where(at >= WIN, turned, 0.0)
                tops[e + 1] = jnp.where(at < WIN, turned, 0.0)
        for e in range(n_tiles):
            cols_ref[e, pl.ds(first, block), :] = tops[e]
        return unused

    lax.fori_loop(0, members // CHUNK, chunk, 0)
    odd, low, high = place()
    for e in range(n_tiles):
        cut = slice(e * LANES, (e + 1) * LANES)
        sums = [None] * (size.rows + 2)
        for i in range(fine_rows):
            value = cols_ref[e, pl.ds(i, members, stride=fine_rows), :]
            for j in range(size.rows + 2):
                weight = tent(i + 0.5 - RATIO * (j - 1) - RATIO / 2)
                if weight:
                    term = value * weight
                    sums[j] = term if sums[j] is None else sums[j] + term
        sums[0] = sums[0] * low
        sums[-1] = sums[-1] * high
        for j in range(size.rows + 2):
            coarse_ref[j * members : (j + 1) * members, cut] = sums[j]
    head = coarse_ref[:, 0:LANES]
    tail = coarse_ref[:, (n_tiles - 1) * LANES :]
    at = lane(head.shape)
    turned_head, turned_tail = half_turn(head), half_turn(tail)
    coarse_ref[:, 0:LANES] = head + jnp.where(at < WIN, turned_tail, 0.0)
    coarse_ref[:, (n_tiles - 1) * LANES :] = tail + jnp.where(at >= WIN, turned_head, 0.0)
    for e in range(n_tiles):
        cut = slice(e * LANES, (e + 1) * LANES)
        for at in range(0, members, 8):
            held = [
                coarse_ref[j * members + at : j * members + at + 8, cut]
                for j in range(size.rows + 2)
            ]
            for k in range(3 * REACH):
                total = None
                for j in range(size.rows + 2):
                    weight = smooth(j - 1 - (k - REACH))
                    if weight:
                        term = held[j] * weight
                        total = term if total is None else total + term
                spread_ref[k * members + at : k * members + at + 8, cut] = total
    n = size.slab

    def packed_of(part):
        tiles = [
            spread_ref[part * n : (part + 1) * n, e * LANES : (e + 1) * LANES]
            for e in range(n_tiles)
        ]
        return pack_slab(size, tiles[0], tiles[-1], tiles[1:-1])

    lower, upper = packed_of(0), packed_of(2)
    own_ref[...] = spread_ref[n : 2 * n, :]
    put_packed(a_ref, [jnp.where(odd, x, y) for x, y in zip(lower, upper)])
    put_packed(b_ref, [jnp.where(odd, y, x) for x, y in zip(lower, upper)])


def gradient_kernel(size, later, *refs):
    refs = list(refs)
    own_ref, b_ref, a_ref, weights_ref = refs[:4]
    refs = refs[4:]
    weights = weights_ref[...]
    if later:
        scal_ref, before_ref = refs.pop(0), refs.pop(0)
        weights = weights - step_length(scal_ref) * before_ref[...]
    grad_ref, packed_ref = refs[:2]
    if later:
        refs[2][...] = weights
    lower, upper = sides(a_ref[...], b_ref[...])
    arrived = unpack_slab(size, lower + upper)
    for e in range(size.ext // LANES):
        cut = slice(e * LANES, (e + 1) * LANES)
        grad_ref[:, cut] = weights[:, cut] + own_ref[:, cut] + arrived[e]
    pack_ref(size, packed_ref, tiles_of(grad_ref, size.ext // LANES))


def own_share_kernel(size, before_ref, image_ref, scal_ref, out_ref, list_ref, shares_ref):
    list_ref[...] = before_ref[...] - step_length(scal_ref) * image_ref[...]
    for q in range(size.n_mem):
        put_share(size, shares_ref.at[q], list_ref, q * size.share)
    out_ref[...] = shares_ref[lax.axis_index("mem")]


def leave_kernel(size, *refs):
    weights_refs, grad_refs = refs[:GROUPS], refs[GROUPS : 2 * GROUPS]
    field_ref, image_ref, scal1_ref = refs[2 * GROUPS : 2 * GROUPS + 3]
    out_weights_ref, out_field_ref = refs[2 * GROUPS + 3 :]
    second = step_length(scal1_ref)
    n_tiles = size.ext // LANES
    for g in range(GROUPS):
        weights = weights_refs[g][...] - second * grad_refs[g][...]
        tiles = [weights[:, e * LANES : (e + 1) * LANES] for e in range(n_tiles)]
        for e in range(n_tiles):
            tile = tiles[e]
            if e + 1 < n_tiles:
                tile = jnp.where(lane(tile.shape) < MARGIN, tiles[e + 1], tile)
            tile = pltpu.roll(tile, LANES - MARGIN, 1)
            start = e * LANES
            width = min(LANES, size.cols - start)
            for r in range(size.rows):
                to = pl.ds(r * size.members + g * size.group, size.group)
                rows = slice(r * size.group, (r + 1) * size.group)
                out_weights_ref[to, start : start + width] = tile[rows, :width]
    field = field_ref[...] - second * image_ref[...]
    start = 0
    for tile, width in share_tiles(size, field):
        for v in range(size.vars):
            rows = slice(v * size.fine_rows, (v + 1) * size.fine_rows)
            out_field_ref[v, :, start : start + width] = tile[rows, :width]
        start += width


def whole():
    return pl.BlockSpec(memory_space=pltpu.VMEM)


def params(limit):
    return pltpu.CompilerParams(vmem_limit_bytes=limit * 1024 * 1024)


def array(*shape):
    return jax.ShapeDtypeStruct(shape, F32)


def call(kernel, outs, *args, scratch=(), flops=0, spaces=None, moved=None, limit=24):
    spaces = spaces or [
        pltpu.MemorySpace.SMEM if arg.ndim == 1 else pltpu.MemorySpace.VMEM for arg in args
    ]
    if moved is None:
        moved = sum(arg.size * arg.dtype.itemsize for arg in args)
    return pl.pallas_call(
        kernel,
        out_shape=outs,
        in_specs=[pl.BlockSpec(memory_space=space) for space in spaces],
        out_specs=jax.tree.map(lambda unused: whole(), outs),
        scratch_shapes=scratch,
        compiler_params=params(limit),
        cost_estimate=pl.CostEstimate(flops=flops, bytes_accessed=moved, transcendentals=0),
    )(*args)


def per_device(mesh, perturbations, control, innovations, thresholds):
    size = Sizes(mesh, perturbations, control)
    n_mem, n_lat, members = size.n_mem, size.n_lat, size.members
    devices = n_mem * n_lat
    pairs = [(i, i ^ 1) for i in range(n_lat)]
    cross = [(i, (i - 1 if i % 2 == 0 else i + 1) % n_lat) for i in range(n_lat)]
    middle_first = sorted(range(1, n_mem), key=lambda d: (d != n_mem // 2, d))
    groups = range(GROUPS)
    slab = array(size.slab, size.ext)
    packed = array(size.packed, LANES)
    part = array(size.part_rows, LANES)
    share = array(size.share_rows, LANES)
    scal = array(devices, LANES)
    field = array(size.list_rows, LANES)
    map_flops = 4 * size.group * size.fine_rows * size.fine_cols * 2 * LANES

    def swap(to_a, to_b):
        return lax.ppermute(to_a, "lat", pairs), lax.ppermute(to_b, "lat", cross)

    def exchange(parts, order):
        return [parts[0]] + [
            lax.ppermute(parts[d], "mem", [(i, i ^ d) for i in range(n_mem)]) for d in order
        ]

    def forward(owns, arrived, *first_step):
        shares = len(first_step) > 0
        acc = []
        piece = share if shares else part
        for g in groups:
            last = g == GROUPS - 1
            scratch = [
                pltpu.VMEM((3 * size.slab, size.ext), F32),
                pltpu.VMEM(((size.rows + 2) * size.group, size.ext), F32),
                pltpu.VMEM((size.windows, size.group * size.fine_rows, LANES), F32),
            ]
            if last:
                scratch.append(pltpu.VMEM(field.shape, F32))
                if shares:
                    scratch.append(pltpu.VMEM((n_mem, *piece.shape), F32))
            outs = [piece] * n_mem if last else [field]
            extra = shares and g == 0
            if extra:
                outs.append(share)
                scratch += [pltpu.VMEM(field.shape, F32), pltpu.VMEM((n_mem, *share.shape), F32)]
            acc = call(
                functools.partial(forward_kernel, size, g, shares),
                outs,
                owns[g],
                *arrived[g][::-1],
                resident,
                *acc,
                *(first_step if extra else ()),
                scratch=scratch,
                flops=map_flops,
            )
            if extra:
                *acc, own_share = acc
        acc = exchange(acc, middle_first)
        return (acc, own_share) if shares else acc

    def adjoint(parts, *step):
        later = len(step) > 0
        sent, spread, misfit, whole_field = [], [], None, None
        for g in groups:
            scratch = [
                pltpu.VMEM((size.ext // LANES, size.group * size.fine_rows, LANES), F32),
                pltpu.VMEM(((size.rows + 2) * size.group, size.ext), F32),
                pltpu.VMEM((3 * size.slab, size.ext), F32),
            ]
            outs = [packed, packed, slab]
            args = [misfit]
            if g == 0:
                outs += [field, field]
                args = [*parts, *step, innovations, thresholds.reshape(1, size.vars)]
            results = call(
                functools.partial(adjoint_kernel, size, g, later),
                outs,
                resident,
                *args,
                scratch=scratch,
                flops=map_flops,
            )
            sent.append(swap(*results[:2]))
            spread.append(results[2])
            if g == 0:
                misfit = results[3]
                whole_field = results[4]
        return sent, spread, whole_field

    def gradient(arrived, spread, weights, *step):
        later = len(step) > 0
        grads, sent, olds = [], [], []
        for g in groups:
            results = call(
                functools.partial(gradient_kernel, size, later),
                [slab, packed] + ([slab] if later else []),
                spread[g],
                *arrived[g][::-1],
                weights[g],
                *([step[0], step[1][g]] if later else []),
            )
            grads.append(results[0])
            sent.append(results[1])
            olds.append(results[2] if later else weights[g])
        return grads, sent, olds

    def squares(parts, sent):
        return call(
            functools.partial(squares_kernel, n_mem),
            [array(*parts[0].shape), scal],
            *parts,
            *sent,
        )

    def everywhere(tile):
        moved = lax.all_to_all(tile.reshape(devices, 1, LANES), ("mem", "lat"), 0, 0)
        return moved.reshape(devices, LANES)

    def both(sent):
        return [swap(x, x) for x in sent]

    entered = call(
        functools.partial(enter_kernel, size),
        [slab, packed] * GROUPS,
        control.transpose(1, 0, 2).reshape(size.rows * members, size.cols),
    )
    control_own, sent = entered[0::2], entered[1::2]
    copies = min(4, members)
    resident = call(
        load_kernel,
        pltpu.VMEM(perturbations.shape, F32),
        pltpu.with_memory_space_constraint(perturbations, pltpu.HBM),
        scratch=[
            pltpu.VMEM(perturbations.shape, perturbations.dtype),
            pltpu.SemaphoreType.DMA((copies,)),
        ],
        spaces=[pltpu.MemorySpace.HBM],
        flops=2 * map_flops,
    )
    parts = forward(control_own, both(sent))
    field0 = call(functools.partial(total_kernel, n_mem), part, *parts)
    arrived, spread, before = adjoint(exchange([field0] * n_mem, size.far_first))
    grads0, sent, unused = gradient(arrived, spread, control_own)
    parts = forward(grads0, both(sent))
    image0, scal0 = squares(parts, sent)
    images = exchange([image0] * n_mem, size.far_first)
    scal0 = everywhere(scal0)
    arrived, spread, image_all = adjoint(images, scal0, before)
    grads1, sent, weights1 = gradient(arrived, spread, control_own, scal0, grads0)
    parts, own_share = forward(grads1, both(sent), before, image_all, scal0)
    image1, scal1 = squares(parts, sent)
    scal1 = everywhere(scal1)
    weights, result = call(
        functools.partial(leave_kernel, size),
        [
            array(size.rows * members, size.cols),
            array(size.vars, size.fine_rows, size.share),
        ],
        *weights1,
        *grads1,
        own_share,
        image1,
        scal1,
    )
    return weights.reshape(size.rows, members, size.cols).transpose(1, 0, 2), result


def solution(mesh):
    return jax.shard_map(
        functools.partial(per_device, mesh),
        mesh=mesh,
        in_specs=(P("mem", None, "lat", None), P("mem", "lat", None), P(None, "lat", None), P()),
        out_specs=(P("mem", "lat", None), P(None, "lat", "mem")),
        check_vma=False,
    )
```

```python
import functools

import jax
import jax.numpy as jnp
from jax import lax
from jax.experimental import pallas as pl
from jax.experimental.pallas import tpu as pltpu
from jax.sharding import PartitionSpec as P

RATIO = 4
HALF = 5
STEPS = 2
REACH = HALF + 1
LANES = 128
WIN = 64
MARGIN = 32
FINE = RATIO * WIN
GROUPS = 2
F32 = jnp.float32
BF16 = jnp.bfloat16


def tent(distance):
    return max(0.0, 1.0 - abs(distance) / RATIO)


def smooth(distance):
    return (1.0 - abs(distance) / REACH) / 2 if abs(distance) <= HALF else 0.0


def window_table(fine_axis, width=LANES):
    shape = (FINE, width) if fine_axis == 0 else (width, FINE)
    fine = lax.broadcasted_iota(jnp.int32, shape, fine_axis).astype(F32)
    coarse = lax.broadcasted_iota(jnp.int32, shape, 1 - fine_axis).astype(F32)
    coarse = coarse - (MARGIN + (width - LANES) // 2)
    distance = fine + 0.5 - RATIO * coarse - RATIO / 2
    table = jnp.maximum(0.0, 1.0 - jnp.abs(distance) / RATIO).astype(BF16)
    return jnp.concatenate([table, table], axis=0)


class Sizes:
    def __init__(self, mesh, perturbations, control):
        self.n_mem = mesh.shape["mem"]
        self.n_lat = mesh.shape["lat"]
        self.far_first = range(self.n_mem - 1, 0, -1)
        self.members = control.shape[0]
        self.group = self.members // GROUPS
        self.rows = control.shape[1]
        self.cols = control.shape[2]
        self.vars = perturbations.shape[1]
        self.fine_rows = perturbations.shape[2]
        self.fine_cols = perturbations.shape[3]
        assert self.rows == REACH and self.cols % LANES == WIN
        assert self.members % (8 * GROUPS) == 0 and self.n_lat % 2 == 0
        assert self.fine_rows == RATIO * self.rows and self.fine_cols == RATIO * self.cols
        self.windows = self.cols // WIN
        self.ext = self.cols + 2 * MARGIN
        self.slab = self.rows * self.group
        self.full = self.cols // LANES
        self.packed = self.full * self.slab + self.slab // 2
        self.field_rows = self.vars * self.fine_rows
        self.share = self.fine_cols // self.n_mem
        self.share_full = self.share // LANES
        self.share_rem = self.share % LANES
        self.groups = LANES // self.share_rem if self.share_rem else 1
        self.rem_rows = -(-self.field_rows // 8 // self.groups) * 8 if self.share_rem else 0
        self.share_rows = self.share_full * self.field_rows + self.rem_rows
        self.field_tiles = self.fine_cols // LANES
        self.part_rows = -(-self.field_tiles * self.field_rows // 8 // self.n_mem) * 8
        self.list_rows = self.part_rows * self.n_mem


def lane(shape):
    return lax.broadcasted_iota(jnp.int32, shape, 1)


def half_turn(x):
    return pltpu.roll(x, WIN, 1)


def pack_slab(size, first, last, middle):
    rows = size.slab
    at = lane((rows, LANES))
    pieces = list(middle)
    pieces.append(jnp.where(at < LANES - MARGIN, last, first))
    half = rows // 2
    at = lane((half, LANES))
    inner = (at >= MARGIN) & (at < LANES - MARGIN)
    pieces.append(jnp.where(inner, first[:half], half_turn(first[half:])))
    return pieces


def unpack_slab(size, packed):
    rows = size.slab
    middle = [packed[i * rows : (i + 1) * rows] for i in range(size.full - 1)]
    mixed = packed[(size.full - 1) * rows : size.full * rows]
    rest = packed[size.full * rows :]
    rest = jnp.concatenate([rest, half_turn(rest)], axis=0)
    at = lane((rows, LANES))
    first = jnp.where(at < MARGIN, half_turn(mixed), jnp.where(at < LANES - MARGIN, rest, mixed))
    last = jnp.where(at < LANES - MARGIN, mixed, half_turn(rest))
    return [first] + middle + [last]


def tiles_of(ref, count):
    return [ref[:, i * LANES : (i + 1) * LANES] for i in range(count)]


def put_packed(out, pieces):
    at = 0
    for piece in pieces:
        out[at : at + piece.shape[0], :] = piece
        at += piece.shape[0]


def pack_ref(size, out, tiles):
    put_packed(out, pack_slab(size, tiles[0], tiles[-1], tiles[1:-1]))


def place():
    lat = lax.axis_index("lat")
    odd = lax.rem(lat, 2) == 1
    low = (lat > 0).astype(F32)
    high = (lat < lax.axis_size("lat") - 1).astype(F32)
    return odd, low, high


def sides(a, b):
    odd, low, high = place()
    lower = jnp.where(odd, a, b) * low
    upper = jnp.where(odd, b, a) * high
    return lower, upper


def step_length(scal_ref):
    total = jnp.sum(scal_ref[...], axis=0, keepdims=True)
    at = lane(total.shape)
    grad_sq = jnp.sum(jnp.where(at == 0, total, 0.0), axis=1, keepdims=True)
    image_sq = jnp.sum(jnp.where(at == 1, total, 0.0), axis=1, keepdims=True)
    return grad_sq / (grad_sq + image_sq)


def enter_kernel(size, control_ref, *outs):
    for g in range(GROUPS):
        own_ref, packed_ref = outs[2 * g : 2 * g + 2]
        x = jnp.concatenate(
            [
                control_ref[pl.ds(r * size.members + g * size.group, size.group), :]
                for r in range(size.rows)
            ],
            axis=0,
        )
        own_ref[...] = jnp.concatenate([x[:, size.cols - MARGIN :], x, x[:, :MARGIN]], axis=1)
        pack_ref(size, packed_ref, tiles_of(own_ref, size.ext // LANES))


def load_kernel(pert_ref, out_ref, held_ref, sems):
    count = sems.shape[0]
    part = pert_ref.shape[0] // count
    copies = [
        pltpu.make_async_copy(
            pert_ref.at[pl.ds(i * part, part)], held_ref.at[pl.ds(i * part, part)], sems.at[i]
        )
        for i in range(count)
    ]
    for copy in copies:
        copy.start()
    for i, copy in enumerate(copies):
        copy.wait()

        def widen(m, unused):
            for v in range(pert_ref.shape[1]):
                out_ref[m, v] = held_ref[m, v].astype(F32)
            return unused

        lax.fori_loop(i * part, (i + 1) * part, widen, 0)


def forward_kernel(size, g, shares, own_ref, b_ref, a_ref, pert_ref, *rest):
    rest = list(rest)
    start_ref = rest.pop(0) if g else None
    last = g == GROUPS - 1
    extra = shares and g == 0
    if extra:
        sources = [rest.pop(0) for i in range(3)]
    outs = [rest.pop(0) for i in range(size.n_mem if last else 1)]
    if extra:
        own_share_kernel(size, *sources, rest.pop(0), *rest[-2:])
    ext_ref, coarse_ref, rows_ref = rest[:3]
    acc_ref = rest[3] if last else outs[0]
    members = size.group
    n_tiles = size.ext // LANES
    fine_rows = size.fine_rows

    unused, low, high = place()
    lower, upper = sides(a_ref[...], b_ref[...])
    lower = unpack_slab(size, lower)
    upper = unpack_slab(size, upper)
    n = size.slab
    for e in range(n_tiles):
        cut = slice(e * LANES, (e + 1) * LANES)
        ext_ref[0:n, cut] = lower[e]
        ext_ref[n : 2 * n, cut] = own_ref[:, cut]
        ext_ref[2 * n : 3 * n, cut] = upper[e]
    for e in range(n_tiles):
        cut = slice(e * LANES, (e + 1) * LANES)
        for at in range(0, members, 8):
            held = [
                ext_ref[k * members + at : k * members + at + 8, cut] for k in range(3 * REACH)
            ]
            for j in range(size.rows + 2):
                total = None
                for k in range(3 * REACH):
                    weight = smooth(j - 1 - (k - REACH))
                    if weight:
                        term = held[k] * weight
                        total = term if total is None else total + term
                if j == 0:
                    total = total * low
                if j == size.rows + 1:
                    total = total * high
                coarse_ref[j * members + at : j * members + at + 8, cut] = total
    for t in range(size.windows):
        e = t // 2
        held = []
        for j in range(size.rows + 2):
            at = slice(j * members, (j + 1) * members)
            value = coarse_ref[at, e * LANES : (e + 1) * LANES]
            if t % 2:
                other = coarse_ref[at, (e + 1) * LANES : (e + 2) * LANES]
                value = half_turn(jnp.where(lane(value.shape) < WIN, other, value))
            held.append(value)
        for i in range(fine_rows):
            total = None
            for j in range(size.rows + 2):
                weight = tent(i + 0.5 - RATIO * (j - 1) - RATIO / 2)
                if weight:
                    term = held[j] * weight
                    total = term if total is None else total + term
            rows_ref[t, pl.ds(i, members, stride=fine_rows), :] = total
    table = window_table(1)
    if g:
        acc_ref[...] = start_ref[...]
    else:
        acc_ref[...] = jnp.zeros_like(acc_ref)
    for t in range(size.windows):
        x = rows_ref[t]
        head = x.astype(BF16)
        tail = (x - head.astype(F32)).astype(BF16)
        refined = jnp.dot(
            jnp.concatenate([head, tail], axis=1), table, preferred_element_type=F32
        )
        for e in range(t * FINE // LANES, (t + 1) * FINE // LANES):
            cut = slice(e * LANES, (e + 1) * LANES)
            here = slice(e * LANES - t * FINE, (e + 1) * LANES - t * FINE)
            rows = [
                pl.ds(e * size.field_rows + v * fine_rows, fine_rows)
                for v in range(size.vars)
            ]
            totals = [acc_ref[at, :] for at in rows]
            for m in range(members):
                value = refined[m * fine_rows : (m + 1) * fine_rows, here]
                for v in range(size.vars):
                    pert = pert_ref[g * members + m, v, :, cut]
                    totals[v] = totals[v] + pert * value
            for v in range(size.vars):
                acc_ref[rows[v], :] = totals[v]
    if not last:
        return
    mine = lax.axis_index("mem")
    if shares:
        parts_ref = rest[4]
        for q in range(size.n_mem):
            put_share(size, parts_ref.at[q], acc_ref, q * size.share)
        for d in range(size.n_mem):
            outs[d][...] = parts_ref[mine ^ d]
    else:
        for d in range(size.n_mem):
            first = pl.multiple_of((mine ^ d) * size.part_rows, 8)
            outs[d][...] = acc_ref[pl.ds(first, size.part_rows), :]


def field_tile(size, list_ref, start):
    e, shift = start // LANES, start % LANES
    rows = size.field_rows
    tile = list_ref[e * rows : (e + 1) * rows, :]
    if shift == 0:
        return tile
    if e + 1 < size.field_tiles:
        other = list_ref[(e + 1) * rows : (e + 2) * rows, :]
        tile = jnp.where(lane(tile.shape) < shift, other, tile)
    return pltpu.roll(tile, LANES - shift, 1)


def put_share(size, out, list_ref, start):
    rows = size.field_rows
    for j in range(size.share_full):
        out[j * rows : (j + 1) * rows, :] = field_tile(size, list_ref, start + j * LANES)
    if size.share_rem:
        tile = field_tile(size, list_ref, start + size.share_full * LANES)
        tile = jnp.where(lane(tile.shape) < size.share_rem, tile, 0.0)
        missing = size.rem_rows * size.groups - rows
        if missing:
            tile = jnp.concatenate([tile, jnp.zeros((missing, LANES), F32)], axis=0)
        total = None
        for g in range(size.groups):
            term = tile[g * size.rem_rows : (g + 1) * size.rem_rows]
            if g:
                term = pltpu.roll(term, g * size.share_rem, 1)
            total = term if total is None else total + term
        out[size.share_full * rows :, :] = total


def share_tiles(size, part):
    rows = size.field_rows
    tiles = [(part[j * rows : (j + 1) * rows], LANES) for j in range(size.share_full)]
    if size.share_rem:
        rest = part[size.share_full * rows :]
        stack = [rest]
        for g in range(1, size.groups):
            stack.append(pltpu.roll(rest, LANES - g * size.share_rem, 1))
        tiles.append((jnp.concatenate(stack, axis=0)[:rows], size.share_rem))
    return tiles


def total_kernel(count, *refs):
    parts, out_ref = refs[:count], refs[count]
    total = parts[0][...]
    for part in parts[1:]:
        total = total + part[...]
    out_ref[...] = total


def squares_kernel(count, *refs):
    parts, grads = refs[:count], refs[count : count + GROUPS]
    out_ref, scal_ref = refs[count + GROUPS :]
    total = parts[0][...]
    for part in parts[1:]:
        total = total + part[...]
    out_ref[...] = total
    image_sq = jnp.sum(total * total)
    grad_sq = sum(jnp.sum(grad[...] * grad[...]) for grad in grads)
    at = lane(scal_ref.shape)
    scal_ref[...] = jnp.where(at == 0, grad_sq, jnp.where(at == 1, image_sq, 0.0))


def misfit_of(size, parts, before_ref, scal_ref, innov_ref, limit_ref, list_ref, misfit_ref):
    fine_rows = size.fine_rows
    mine = lax.axis_index("mem")
    for i, d in enumerate((0, *size.far_first)):
        first = pl.multiple_of((mine ^ d) * size.part_rows, 8)
        list_ref[pl.ds(first, size.part_rows), :] = parts[i][...]
    if before_ref is not None:
        length = step_length(scal_ref)
    for e in range(size.field_tiles):
        cut = slice(e * LANES, (e + 1) * LANES)
        for v in range(size.vars):
            at = pl.ds(e * size.field_rows + v * fine_rows, fine_rows)
            value = list_ref[at, :]
            if before_ref is not None:
                value = before_ref[at, :] - length * value
            limit = limit_ref[:, v : v + 1]
            misfit_ref[at, :] = jnp.clip(value - innov_ref[v, :, cut], -limit, limit)


def adjoint_kernel(size, g, later, *refs):
    refs = list(refs)
    pert_ref = refs.pop(0)
    if g == 0:
        parts = [refs.pop(0) for i in range(size.n_mem)]
        scal_ref, before_ref = (refs.pop(0), refs.pop(0)) if later else (None, None)
        innov_ref, limit_ref = refs.pop(0), refs.pop(0)
    else:
        misfit_ref = refs.pop(0)
    a_ref, b_ref, own_ref = refs[:3]
    refs = refs[3:]
    if g == 0:
        misfit_ref = refs.pop(0)
        list_ref = refs.pop(0)
    cols_ref, coarse_ref, spread_ref, held_ref = refs[:4]
    members = size.group
    n_tiles = size.ext // LANES
    fine_rows = size.fine_rows
    if g == 0:
        misfit_of(size, parts, before_ref, scal_ref, innov_ref, limit_ref, list_ref, misfit_ref)
    tables = [window_table(0), window_table(0, 2 * LANES)]

    def weighted(t):
        cut = slice(t * FINE, (t + 1) * FINE)
        tiles = range(t * FINE // LANES, (t + 1) * FINE // LANES)
        mis = [
            jnp.concatenate(
                [
                    misfit_ref[pl.ds(e * size.field_rows + v * fine_rows, fine_rows), :]
                    for e in tiles
                ],
                axis=1,
            )
            for v in range(size.vars)
        ]
        rows = []
        for m in range(members):
            total = pert_ref[g * members + m, 0, :, cut] * mis[0]
            for v in range(1, size.vars):
                total = total + pert_ref[g * members + m, v, :, cut] * mis[v]
            rows.append(total)
        x = jnp.concatenate(rows, axis=0)
        head = x.astype(BF16)
        tail = (x - head.astype(F32)).astype(BF16)
        held_ref[t, :, :FINE] = head
        held_ref[t, :, FINE:] = tail

    def place_columns(t):
        columns = jnp.dot(held_ref[t], tables[t % 2], preferred_element_type=F32)
        e = t // 2
        if t % 2 == 0:
            cols_ref[e] = cols_ref[e] + columns if t else columns
        else:
            cols_ref[e] = cols_ref[e] + columns[:, :LANES]
            cols_ref[e + 1] = columns[:, LANES:]

    weighted(0)
    for t in range(size.windows):
        if t + 1 < size.windows:
            weighted(t + 1)
        place_columns(t)
    odd, low, high = place()
    for e in range(n_tiles):
        cut = slice(e * LANES, (e + 1) * LANES)
        sums = [None] * (size.rows + 2)
        for i in range(fine_rows):
            value = cols_ref[e, pl.ds(i, members, stride=fine_rows), :]
            for j in range(size.rows + 2):
                weight = tent(i + 0.5 - RATIO * (j - 1) - RATIO / 2)
                if weight:
                    term = value * weight
                    sums[j] = term if sums[j] is None else sums[j] + term
        sums[0] = sums[0] * low
        sums[-1] = sums[-1] * high
        for j in range(size.rows + 2):
            coarse_ref[j * members : (j + 1) * members, cut] = sums[j]
    head = coarse_ref[:, 0:LANES]
    tail = coarse_ref[:, (n_tiles - 1) * LANES :]
    at = lane(head.shape)
    turned_head, turned_tail = half_turn(head), half_turn(tail)
    coarse_ref[:, 0:LANES] = head + jnp.where(at < WIN, turned_tail, 0.0)
    coarse_ref[:, (n_tiles - 1) * LANES :] = tail + jnp.where(at >= WIN, turned_head, 0.0)
    for e in range(n_tiles):
        cut = slice(e * LANES, (e + 1) * LANES)
        for at in range(0, members, 8):
            held = [
                coarse_ref[j * members + at : j * members + at + 8, cut]
                for j in range(size.rows + 2)
            ]
            for k in range(3 * REACH):
                total = None
                for j in range(size.rows + 2):
                    weight = smooth(j - 1 - (k - REACH))
                    if weight:
                        term = held[j] * weight
                        total = term if total is None else total + term
                spread_ref[k * members + at : k * members + at + 8, cut] = total
    n = size.slab

    def packed_of(part):
        tiles = [
            spread_ref[part * n : (part + 1) * n, e * LANES : (e + 1) * LANES]
            for e in range(n_tiles)
        ]
        return pack_slab(size, tiles[0], tiles[-1], tiles[1:-1])

    lower, upper = packed_of(0), packed_of(2)
    own_ref[...] = spread_ref[n : 2 * n, :]
    put_packed(a_ref, [jnp.where(odd, x, y) for x, y in zip(lower, upper)])
    put_packed(b_ref, [jnp.where(odd, y, x) for x, y in zip(lower, upper)])


def gradient_kernel(size, later, *refs):
    refs = list(refs)
    own_ref, b_ref, a_ref, weights_ref = refs[:4]
    refs = refs[4:]
    weights = weights_ref[...]
    if later:
        scal_ref, before_ref = refs.pop(0), refs.pop(0)
        weights = weights - step_length(scal_ref) * before_ref[...]
    grad_ref, packed_ref = refs[:2]
    if later:
        refs[2][...] = weights
    lower, upper = sides(a_ref[...], b_ref[...])
    arrived = unpack_slab(size, lower + upper)
    for e in range(size.ext // LANES):
        cut = slice(e * LANES, (e + 1) * LANES)
        grad_ref[:, cut] = weights[:, cut] + own_ref[:, cut] + arrived[e]
    pack_ref(size, packed_ref, tiles_of(grad_ref, size.ext // LANES))


def own_share_kernel(size, before_ref, image_ref, scal_ref, out_ref, list_ref, shares_ref):
    list_ref[...] = before_ref[...] - step_length(scal_ref) * image_ref[...]
    for q in range(size.n_mem):
        put_share(size, shares_ref.at[q], list_ref, q * size.share)
    out_ref[...] = shares_ref[lax.axis_index("mem")]


def leave_kernel(size, *refs):
    weights_refs, grad_refs = refs[:GROUPS], refs[GROUPS : 2 * GROUPS]
    field_ref, image_ref, scal1_ref = refs[2 * GROUPS : 2 * GROUPS + 3]
    out_weights_ref, out_field_ref = refs[2 * GROUPS + 3 :]
    second = step_length(scal1_ref)
    n_tiles = size.ext // LANES
    for g in range(GROUPS):
        weights = weights_refs[g][...] - second * grad_refs[g][...]
        tiles = [weights[:, e * LANES : (e + 1) * LANES] for e in range(n_tiles)]
        for e in range(n_tiles):
            tile = tiles[e]
            if e + 1 < n_tiles:
                tile = jnp.where(lane(tile.shape) < MARGIN, tiles[e + 1], tile)
            tile = pltpu.roll(tile, LANES - MARGIN, 1)
            start = e * LANES
            width = min(LANES, size.cols - start)
            for r in range(size.rows):
                to = pl.ds(r * size.members + g * size.group, size.group)
                rows = slice(r * size.group, (r + 1) * size.group)
                out_weights_ref[to, start : start + width] = tile[rows, :width]
    field = field_ref[...] - second * image_ref[...]
    start = 0
    for tile, width in share_tiles(size, field):
        for v in range(size.vars):
            rows = slice(v * size.fine_rows, (v + 1) * size.fine_rows)
            out_field_ref[v, :, start : start + width] = tile[rows, :width]
        start += width


def whole():
    return pl.BlockSpec(memory_space=pltpu.VMEM)


def params(limit):
    return pltpu.CompilerParams(vmem_limit_bytes=limit * 1024 * 1024)


def array(*shape):
    return jax.ShapeDtypeStruct(shape, F32)


def call(kernel, outs, *args, scratch=(), flops=0, spaces=None, moved=None, limit=24):
    spaces = spaces or [
        pltpu.MemorySpace.SMEM if arg.ndim == 1 else pltpu.MemorySpace.VMEM for arg in args
    ]
    if moved is None:
        moved = sum(arg.size * arg.dtype.itemsize for arg in args)
    return pl.pallas_call(
        kernel,
        out_shape=outs,
        in_specs=[pl.BlockSpec(memory_space=space) for space in spaces],
        out_specs=jax.tree.map(lambda unused: whole(), outs),
        scratch_shapes=scratch,
        compiler_params=params(limit),
        cost_estimate=pl.CostEstimate(flops=flops, bytes_accessed=moved, transcendentals=0),
    )(*args)


def per_device(mesh, perturbations, control, innovations, thresholds):
    size = Sizes(mesh, perturbations, control)
    n_mem, n_lat, members = size.n_mem, size.n_lat, size.members
    devices = n_mem * n_lat
    pairs = [(i, i ^ 1) for i in range(n_lat)]
    cross = [(i, (i - 1 if i % 2 == 0 else i + 1) % n_lat) for i in range(n_lat)]
    middle_first = sorted(range(1, n_mem), key=lambda d: (d != n_mem // 2, d))
    groups = range(GROUPS)
    slab = array(size.slab, size.ext)
    packed = array(size.packed, LANES)
    part = array(size.part_rows, LANES)
    share = array(size.share_rows, LANES)
    scal = array(devices, LANES)
    field = array(size.list_rows, LANES)
    map_flops = 4 * size.group * size.fine_rows * size.fine_cols * 2 * LANES

    def swap(to_a, to_b):
        return lax.ppermute(to_a, "lat", pairs), lax.ppermute(to_b, "lat", cross)

    def exchange(parts, order):
        return [parts[0]] + [
            lax.ppermute(parts[d], "mem", [(i, i ^ d) for i in range(n_mem)]) for d in order
        ]

    def forward(order, owns, arrived, *first_step):
        shares = len(first_step) > 0
        acc = []
        piece = share if shares else part
        for g in groups:
            last = g == GROUPS - 1
            scratch = [
                pltpu.VMEM((3 * size.slab, size.ext), F32),
                pltpu.VMEM(((size.rows + 2) * size.group, size.ext), F32),
                pltpu.VMEM((size.windows, size.group * size.fine_rows, LANES), F32),
            ]
            if last:
                scratch.append(pltpu.VMEM(field.shape, F32))
                if shares:
                    scratch.append(pltpu.VMEM((n_mem, *piece.shape), F32))
            outs = [piece] * n_mem if last else [field]
            extra = shares and g == 0
            if extra:
                outs.append(share)
                scratch += [pltpu.VMEM(field.shape, F32), pltpu.VMEM((n_mem, *share.shape), F32)]
            acc = call(
                functools.partial(forward_kernel, size, g, shares),
                outs,
                owns[g],
                *arrived[g][::-1],
                resident,
                *acc,
                *(first_step if extra else ()),
                scratch=scratch,
                flops=map_flops,
            )
            if extra:
                *acc, own_share = acc
        acc = exchange(acc, order)
        return (acc, own_share) if shares else acc

    def adjoint(parts, *step):
        later = len(step) > 0
        sent, spread, misfit, whole_field = [], [], None, None
        for g in groups:
            scratch = [
                pltpu.VMEM((size.ext // LANES, size.group * size.fine_rows, LANES), F32),
                pltpu.VMEM(((size.rows + 2) * size.group, size.ext), F32),
                pltpu.VMEM((3 * size.slab, size.ext), F32),
                pltpu.VMEM((size.windows, size.group * size.fine_rows, 2 * FINE), BF16),
            ]
            outs = [packed, packed, slab]
            args = [misfit]
            if g == 0:
                outs += [field, field]
                args = [*parts, *step, innovations, thresholds.reshape(1, size.vars)]
            results = call(
                functools.partial(adjoint_kernel, size, g, later),
                outs,
                resident,
                *args,
                scratch=scratch,
                flops=map_flops,
            )
            sent.append(swap(*results[:2]))
            spread.append(results[2])
            if g == 0:
                misfit = results[3]
                whole_field = results[4]
        return sent, spread, whole_field

    def gradient(arrived, spread, weights, *step):
        later = len(step) > 0
        grads, sent, olds = [], [], []
        for g in groups:
            results = call(
                functools.partial(gradient_kernel, size, later),
                [slab, packed] + ([slab] if later else []),
                spread[g],
                *arrived[g][::-1],
                weights[g],
                *([step[0], step[1][g]] if later else []),
            )
            grads.append(results[0])
            sent.append(results[1])
            olds.append(results[2] if later else weights[g])
        return grads, sent, olds

    def squares(parts, sent):
        return call(
            functools.partial(squares_kernel, n_mem),
            [array(*parts[0].shape), scal],
            *parts,
            *sent,
        )

    def everywhere(tile):
        moved = lax.all_to_all(tile.reshape(devices, 1, LANES), ("mem", "lat"), 0, 0)
        return moved.reshape(devices, LANES)

    def both(sent):
        return [swap(x, x) for x in sent]

    entered = call(
        functools.partial(enter_kernel, size),
        [slab, packed] * GROUPS,
        control.transpose(1, 0, 2).reshape(size.rows * members, size.cols),
    )
    control_own, sent = entered[0::2], entered[1::2]
    copies = min(4, members)
    resident = call(
        load_kernel,
        pltpu.VMEM(perturbations.shape, F32),
        pltpu.with_memory_space_constraint(perturbations, pltpu.HBM),
        scratch=[
            pltpu.VMEM(perturbations.shape, perturbations.dtype),
            pltpu.SemaphoreType.DMA((copies,)),
        ],
        spaces=[pltpu.MemorySpace.HBM],
        flops=2 * map_flops,
    )
    parts = forward(size.far_first, control_own, both(sent))
    field0 = call(functools.partial(total_kernel, n_mem), part, *parts)
    arrived, spread, before = adjoint(exchange([field0] * n_mem, size.far_first))
    grads0, sent, unused = gradient(arrived, spread, control_own)
    parts = forward(middle_first, grads0, both(sent))
    image0, scal0 = squares(parts, sent)
    images = exchange([image0] * n_mem, size.far_first)
    scal0 = everywhere(scal0)
    arrived, spread, image_all = adjoint(images, scal0, before)
    grads1, sent, weights1 = gradient(arrived, spread, control_own, scal0, grads0)
    parts, own_share = forward(middle_first, grads1, both(sent), before, image_all, scal0)
    image1, scal1 = squares(parts, sent)
    scal1 = everywhere(scal1)
    weights, result = call(
        functools.partial(leave_kernel, size),
        [
            array(size.rows * members, size.cols),
            array(size.vars, size.fine_rows, size.share),
        ],
        *weights1,
        *grads1,
        own_share,
        image1,
        scal1,
    )
    return weights.reshape(size.rows, members, size.cols).transpose(1, 0, 2), result


def solution(mesh):
    return jax.shard_map(
        functools.partial(per_device, mesh),
        mesh=mesh,
        in_specs=(P("mem", None, "lat", None), P("mem", "lat", None), P(None, "lat", None), P()),
        out_specs=(P("mem", "lat", None), P(None, "lat", "mem")),
        check_vma=False,
    )
```

```python
import functools

import jax
import jax.numpy as jnp
from jax import lax
from jax.experimental import pallas as pl
from jax.experimental.pallas import tpu as pltpu
from jax.sharding import PartitionSpec as P

RATIO = 4
HALF = 5
STEPS = 2
REACH = HALF + 1
LANES = 128
WIN = 64
MARGIN = 32
FINE = RATIO * WIN
GROUPS = 2
F32 = jnp.float32
BF16 = jnp.bfloat16


def tent(distance):
    return max(0.0, 1.0 - abs(distance) / RATIO)


def smooth(distance):
    return (1.0 - abs(distance) / REACH) / 2 if abs(distance) <= HALF else 0.0


def window_table(fine_axis, width=LANES):
    shape = (FINE, width) if fine_axis == 0 else (width, FINE)
    fine = lax.broadcasted_iota(jnp.int32, shape, fine_axis).astype(F32)
    coarse = lax.broadcasted_iota(jnp.int32, shape, 1 - fine_axis).astype(F32)
    coarse = coarse - (MARGIN + (width - LANES) // 2)
    distance = fine + 0.5 - RATIO * coarse - RATIO / 2
    table = jnp.maximum(0.0, 1.0 - jnp.abs(distance) / RATIO).astype(BF16)
    return jnp.concatenate([table, table], axis=0)


class Sizes:
    def __init__(self, mesh, perturbations, control):
        self.n_mem = mesh.shape["mem"]
        self.n_lat = mesh.shape["lat"]
        self.far_first = range(self.n_mem - 1, 0, -1)
        self.members = control.shape[0]
        self.group = self.members // GROUPS
        self.rows = control.shape[1]
        self.cols = control.shape[2]
        self.vars = perturbations.shape[1]
        self.fine_rows = perturbations.shape[2]
        self.fine_cols = perturbations.shape[3]
        assert self.rows == REACH and self.cols % LANES == WIN
        assert self.members % (8 * GROUPS) == 0 and self.n_lat % 2 == 0
        assert self.fine_rows == RATIO * self.rows and self.fine_cols == RATIO * self.cols
        self.windows = self.cols // WIN
        self.ext = self.cols + 2 * MARGIN
        self.slab = self.rows * self.group
        self.full = self.cols // LANES
        self.packed = self.full * self.slab + self.slab // 2
        self.field_rows = self.vars * self.fine_rows
        self.share = self.fine_cols // self.n_mem
        self.share_full = self.share // LANES
        self.share_rem = self.share % LANES
        self.groups = LANES // self.share_rem if self.share_rem else 1
        self.rem_rows = -(-self.field_rows // 8 // self.groups) * 8 if self.share_rem else 0
        self.share_rows = self.share_full * self.field_rows + self.rem_rows
        self.field_tiles = self.fine_cols // LANES
        self.part_rows = -(-self.field_tiles * self.field_rows // 8 // self.n_mem) * 8
        self.list_rows = self.part_rows * self.n_mem


def lane(shape):
    return lax.broadcasted_iota(jnp.int32, shape, 1)


def half_turn(x):
    return pltpu.roll(x, WIN, 1)


def pack_slab(size, first, last, middle):
    rows = size.slab
    at = lane((rows, LANES))
    pieces = list(middle)
    pieces.append(jnp.where(at < LANES - MARGIN, last, first))
    half = rows // 2
    at = lane((half, LANES))
    inner = (at >= MARGIN) & (at < LANES - MARGIN)
    pieces.append(jnp.where(inner, first[:half], half_turn(first[half:])))
    return pieces


def unpack_slab(size, packed):
    rows = size.slab
    middle = [packed[i * rows : (i + 1) * rows] for i in range(size.full - 1)]
    mixed = packed[(size.full - 1) * rows : size.full * rows]
    rest = packed[size.full * rows :]
    rest = jnp.concatenate([rest, half_turn(rest)], axis=0)
    at = lane((rows, LANES))
    first = jnp.where(at < MARGIN, half_turn(mixed), jnp.where(at < LANES - MARGIN, rest, mixed))
    last = jnp.where(at < LANES - MARGIN, mixed, half_turn(rest))
    return [first] + middle + [last]


def tiles_of(ref, count):
    return [ref[:, i * LANES : (i + 1) * LANES] for i in range(count)]


def put_packed(out, pieces):
    at = 0
    for piece in pieces:
        out[at : at + piece.shape[0], :] = piece
        at += piece.shape[0]


def pack_ref(size, out, tiles):
    put_packed(out, pack_slab(size, tiles[0], tiles[-1], tiles[1:-1]))


def place():
    lat = lax.axis_index("lat")
    odd = lax.rem(lat, 2) == 1
    low = (lat > 0).astype(F32)
    high = (lat < lax.axis_size("lat") - 1).astype(F32)
    return odd, low, high


def sides(a, b):
    odd, low, high = place()
    lower = jnp.where(odd, a, b) * low
    upper = jnp.where(odd, b, a) * high
    return lower, upper


def step_length(scal_ref):
    total = jnp.sum(scal_ref[...], axis=0, keepdims=True)
    at = lane(total.shape)
    grad_sq = jnp.sum(jnp.where(at == 0, total, 0.0), axis=1, keepdims=True)
    image_sq = jnp.sum(jnp.where(at == 1, total, 0.0), axis=1, keepdims=True)
    return grad_sq / (grad_sq + image_sq)


def enter_kernel(size, control_ref, *outs):
    for g in range(GROUPS):
        own_ref, packed_ref = outs[2 * g : 2 * g + 2]
        x = jnp.concatenate(
            [
                control_ref[pl.ds(r * size.members + g * size.group, size.group), :]
                for r in range(size.rows)
            ],
            axis=0,
        )
        own_ref[...] = jnp.concatenate([x[:, size.cols - MARGIN :], x, x[:, :MARGIN]], axis=1)
        pack_ref(size, packed_ref, tiles_of(own_ref, size.ext // LANES))


def load_kernel(pert_ref, out_ref, held_ref, sems):
    count = sems.shape[0]
    part = pert_ref.shape[0] // count
    copies = [
        pltpu.make_async_copy(
            pert_ref.at[pl.ds(i * part, part)], held_ref.at[pl.ds(i * part, part)], sems.at[i]
        )
        for i in range(count)
    ]
    for copy in copies:
        copy.start()
    for i, copy in enumerate(copies):
        copy.wait()

        def widen(m, unused):
            for v in range(pert_ref.shape[1]):
                out_ref[m, v] = held_ref[m, v].astype(F32)
            return unused

        lax.fori_loop(i * part, (i + 1) * part, widen, 0)


def forward_kernel(size, g, shares, own_ref, b_ref, a_ref, pert_ref, *rest):
    rest = list(rest)
    start_ref = rest.pop(0) if g else None
    last = g == GROUPS - 1
    extra = shares and g == 0
    if extra:
        sources = [rest.pop(0) for i in range(3)]
    outs = [rest.pop(0) for i in range(size.n_mem if last else 1)]
    if extra:
        own_share_kernel(size, *sources, rest.pop(0), *rest[-2:])
    ext_ref, coarse_ref, rows_ref = rest[:3]
    acc_ref = rest[3] if last else outs[0]
    members = size.group
    n_tiles = size.ext // LANES
    fine_rows = size.fine_rows

    unused, low, high = place()
    lower, upper = sides(a_ref[...], b_ref[...])
    lower = unpack_slab(size, lower)
    upper = unpack_slab(size, upper)
    n = size.slab
    for e in range(n_tiles):
        cut = slice(e * LANES, (e + 1) * LANES)
        ext_ref[0:n, cut] = lower[e]
        ext_ref[n : 2 * n, cut] = own_ref[:, cut]
        ext_ref[2 * n : 3 * n, cut] = upper[e]
    for e in range(n_tiles):
        cut = slice(e * LANES, (e + 1) * LANES)
        for at in range(0, members, 8):
            held = [
                ext_ref[k * members + at : k * members + at + 8, cut] for k in range(3 * REACH)
            ]
            for j in range(size.rows + 2):
                total = None
                for k in range(3 * REACH):
                    weight = smooth(j - 1 - (k - REACH))
                    if weight:
                        term = held[k] * weight
                        total = term if total is None else total + term
                if j == 0:
                    total = total * low
                if j == size.rows + 1:
                    total = total * high
                coarse_ref[j * members + at : j * members + at + 8, cut] = total
    for t in range(size.windows):
        e = t // 2
        held = []
        for j in range(size.rows + 2):
            at = slice(j * members, (j + 1) * members)
            value = coarse_ref[at, e * LANES : (e + 1) * LANES]
            if t % 2:
                other = coarse_ref[at, (e + 1) * LANES : (e + 2) * LANES]
                value = half_turn(jnp.where(lane(value.shape) < WIN, other, value))
            held.append(value)
        for i in range(fine_rows):
            total = None
            for j in range(size.rows + 2):
                weight = tent(i + 0.5 - RATIO * (j - 1) - RATIO / 2)
                if weight:
                    term = held[j] * weight
                    total = term if total is None else total + term
            rows_ref[t, pl.ds(i, members, stride=fine_rows), :] = total
    table = window_table(1)
    if g:
        acc_ref[...] = start_ref[...]
    else:
        acc_ref[...] = jnp.zeros_like(acc_ref)
    for t in range(size.windows):
        x = rows_ref[t]
        head = x.astype(BF16)
        tail = (x - head.astype(F32)).astype(BF16)
        refined = jnp.dot(
            jnp.concatenate([head, tail], axis=1), table, preferred_element_type=F32
        )
        for e in range(t * FINE // LANES, (t + 1) * FINE // LANES):
            cut = slice(e * LANES, (e + 1) * LANES)
            here = slice(e * LANES - t * FINE, (e + 1) * LANES - t * FINE)
            rows = [
                pl.ds(e * size.field_rows + v * fine_rows, fine_rows)
                for v in range(size.vars)
            ]
            totals = [acc_ref[at, :] for at in rows]
            for m in range(members):
                value = refined[m * fine_rows : (m + 1) * fine_rows, here]
                for v in range(size.vars):
                    pert = pert_ref[g * members + m, v, :, cut]
                    totals[v] = totals[v] + pert * value
            for v in range(size.vars):
                acc_ref[rows[v], :] = totals[v]
    if not last:
        return
    mine = lax.axis_index("mem")
    if shares:
        parts_ref = rest[4]
        for q in range(size.n_mem):
            put_share(size, parts_ref.at[q], acc_ref, q * size.share)
        for d in range(size.n_mem):
            outs[d][...] = parts_ref[mine ^ d]
    else:
        for d in range(size.n_mem):
            first = pl.multiple_of((mine ^ d) * size.part_rows, 8)
            outs[d][...] = acc_ref[pl.ds(first, size.part_rows), :]


def field_tile(size, list_ref, start):
    e, shift = start // LANES, start % LANES
    rows = size.field_rows
    tile = list_ref[e * rows : (e + 1) * rows, :]
    if shift == 0:
        return tile
    if e + 1 < size.field_tiles:
        other = list_ref[(e + 1) * rows : (e + 2) * rows, :]
        tile = jnp.where(lane(tile.shape) < shift, other, tile)
    return pltpu.roll(tile, LANES - shift, 1)


def put_share(size, out, list_ref, start):
    rows = size.field_rows
    for j in range(size.share_full):
        out[j * rows : (j + 1) * rows, :] = field_tile(size, list_ref, start + j * LANES)
    if size.share_rem:
        tile = field_tile(size, list_ref, start + size.share_full * LANES)
        tile = jnp.where(lane(tile.shape) < size.share_rem, tile, 0.0)
        missing = size.rem_rows * size.groups - rows
        if missing:
            tile = jnp.concatenate([tile, jnp.zeros((missing, LANES), F32)], axis=0)
        total = None
        for g in range(size.groups):
            term = tile[g * size.rem_rows : (g + 1) * size.rem_rows]
            if g:
                term = pltpu.roll(term, g * size.share_rem, 1)
            total = term if total is None else total + term
        out[size.share_full * rows :, :] = total


def share_tiles(size, part):
    rows = size.field_rows
    tiles = [(part[j * rows : (j + 1) * rows], LANES) for j in range(size.share_full)]
    if size.share_rem:
        rest = part[size.share_full * rows :]
        stack = [rest]
        for g in range(1, size.groups):
            stack.append(pltpu.roll(rest, LANES - g * size.share_rem, 1))
        tiles.append((jnp.concatenate(stack, axis=0)[:rows], size.share_rem))
    return tiles


def total_kernel(count, *refs):
    parts, out_ref = refs[:count], refs[count]
    total = parts[0][...]
    for part in parts[1:]:
        total = total + part[...]
    out_ref[...] = total


def squares_kernel(count, *refs):
    parts, grads = refs[:count], refs[count : count + GROUPS]
    out_ref, scal_ref = refs[count + GROUPS :]
    total = parts[0][...]
    for part in parts[1:]:
        total = total + part[...]
    out_ref[...] = total
    image_sq = jnp.sum(total * total)
    grad_sq = sum(jnp.sum(grad[...] * grad[...]) for grad in grads)
    at = lane(scal_ref.shape)
    scal_ref[...] = jnp.where(at == 0, grad_sq, jnp.where(at == 1, image_sq, 0.0))


def misfit_of(size, parts, before_ref, scal_ref, innov_ref, limit_ref, list_ref, misfit_ref):
    fine_rows = size.fine_rows
    mine = lax.axis_index("mem")
    for i, d in enumerate((0, *size.far_first)):
        first = pl.multiple_of((mine ^ d) * size.part_rows, 8)
        list_ref[pl.ds(first, size.part_rows), :] = parts[i][...]
    if before_ref is not None:
        length = step_length(scal_ref)
    for e in range(size.field_tiles):
        cut = slice(e * LANES, (e + 1) * LANES)
        for v in range(size.vars):
            at = pl.ds(e * size.field_rows + v * fine_rows, fine_rows)
            value = list_ref[at, :]
            if before_ref is not None:
                value = before_ref[at, :] - length * value
            limit = limit_ref[:, v : v + 1]
            misfit_ref[at, :] = jnp.clip(value - innov_ref[v, :, cut], -limit, limit)


def adjoint_kernel(size, g, later, *refs):
    refs = list(refs)
    pert_ref = refs.pop(0)
    if g == 0:
        parts = [refs.pop(0) for i in range(size.n_mem)]
        scal_ref, before_ref = (refs.pop(0), refs.pop(0)) if later else (None, None)
        innov_ref, limit_ref = refs.pop(0), refs.pop(0)
    else:
        misfit_ref = refs.pop(0)
    a_ref, b_ref, own_ref = refs[:3]
    refs = refs[3:]
    if g == 0:
        misfit_ref = refs.pop(0)
        list_ref = refs.pop(0)
    cols_ref, coarse_ref, spread_ref, held_ref = refs[:4]
    members = size.group
    n_tiles = size.ext // LANES
    fine_rows = size.fine_rows
    if g == 0:
        misfit_of(size, parts, before_ref, scal_ref, innov_ref, limit_ref, list_ref, misfit_ref)
    tables = [window_table(0), window_table(0, 2 * LANES)]

    def weighted(t):
        cut = slice(t * FINE, (t + 1) * FINE)
        tiles = range(t * FINE // LANES, (t + 1) * FINE // LANES)
        mis = [
            jnp.concatenate(
                [
                    misfit_ref[pl.ds(e * size.field_rows + v * fine_rows, fine_rows), :]
                    for e in tiles
                ],
                axis=1,
            )
            for v in range(size.vars)
        ]
        rows = []
        for m in range(members):
            total = pert_ref[g * members + m, 0, :, cut] * mis[0]
            for v in range(1, size.vars):
                total = total + pert_ref[g * members + m, v, :, cut] * mis[v]
            rows.append(total)
        x = jnp.concatenate(rows, axis=0)
        head = x.astype(BF16)
        tail = (x - head.astype(F32)).astype(BF16)
        held_ref[t, :, :FINE] = head
        held_ref[t, :, FINE:] = tail

    def place_columns(t):
        columns = jnp.dot(held_ref[t], tables[t % 2], preferred_element_type=F32)
        e = t // 2
        if t % 2 == 0:
            cols_ref[e] = cols_ref[e] + columns if t else columns
        else:
            cols_ref[e] = cols_ref[e] + columns[:, :LANES]
            cols_ref[e + 1] = columns[:, LANES:]

    weighted(0)
    for t in range(size.windows):
        if t + 1 < size.windows:
            weighted(t + 1)
        place_columns(t)
    odd, low, high = place()
    for e in range(n_tiles):
        cut = slice(e * LANES, (e + 1) * LANES)
        sums = [None] * (size.rows + 2)
        for i in range(fine_rows):
            value = cols_ref[e, pl.ds(i, members, stride=fine_rows), :]
            for j in range(size.rows + 2):
                weight = tent(i + 0.5 - RATIO * (j - 1) - RATIO / 2)
                if weight:
                    term = value * weight
                    sums[j] = term if sums[j] is None else sums[j] + term
        sums[0] = sums[0] * low
        sums[-1] = sums[-1] * high
        for j in range(size.rows + 2):
            coarse_ref[j * members : (j + 1) * members, cut] = sums[j]
    head = coarse_ref[:, 0:LANES]
    tail = coarse_ref[:, (n_tiles - 1) * LANES :]
    at = lane(head.shape)
    turned_head, turned_tail = half_turn(head), half_turn(tail)
    coarse_ref[:, 0:LANES] = head + jnp.where(at < WIN, turned_tail, 0.0)
    coarse_ref[:, (n_tiles - 1) * LANES :] = tail + jnp.where(at >= WIN, turned_head, 0.0)
    for e in range(n_tiles):
        cut = slice(e * LANES, (e + 1) * LANES)
        for at in range(0, members, 8):
            held = [
                coarse_ref[j * members + at : j * members + at + 8, cut]
                for j in range(size.rows + 2)
            ]
            for k in range(3 * REACH):
                total = None
                for j in range(size.rows + 2):
                    weight = smooth(j - 1 - (k - REACH))
                    if weight:
                        term = held[j] * weight
                        total = term if total is None else total + term
                spread_ref[k * members + at : k * members + at + 8, cut] = total
    n = size.slab

    def packed_of(part):
        tiles = [
            spread_ref[part * n : (part + 1) * n, e * LANES : (e + 1) * LANES]
            for e in range(n_tiles)
        ]
        return pack_slab(size, tiles[0], tiles[-1], tiles[1:-1])

    lower, upper = packed_of(0), packed_of(2)
    own_ref[...] = spread_ref[n : 2 * n, :]
    put_packed(a_ref, [jnp.where(odd, x, y) for x, y in zip(lower, upper)])
    put_packed(b_ref, [jnp.where(odd, y, x) for x, y in zip(lower, upper)])


def gradient_kernel(size, later, *refs):
    refs = list(refs)
    own_ref, b_ref, a_ref, weights_ref = refs[:4]
    refs = refs[4:]
    weights = weights_ref[...]
    if later:
        scal_ref, before_ref = refs.pop(0), refs.pop(0)
        weights = weights - step_length(scal_ref) * before_ref[...]
    grad_ref, packed_ref = refs[:2]
    if later:
        refs[2][...] = weights
    lower, upper = sides(a_ref[...], b_ref[...])
    arrived = unpack_slab(size, lower + upper)
    for e in range(size.ext // LANES):
        cut = slice(e * LANES, (e + 1) * LANES)
        grad_ref[:, cut] = weights[:, cut] + own_ref[:, cut] + arrived[e]
    pack_ref(size, packed_ref, tiles_of(grad_ref, size.ext // LANES))


def own_share_kernel(size, before_ref, image_ref, scal_ref, out_ref, list_ref, shares_ref):
    list_ref[...] = before_ref[...] - step_length(scal_ref) * image_ref[...]
    for q in range(size.n_mem):
        put_share(size, shares_ref.at[q], list_ref, q * size.share)
    out_ref[...] = shares_ref[lax.axis_index("mem")]


def leave_kernel(size, *refs):
    weights_refs, grad_refs = refs[:GROUPS], refs[GROUPS : 2 * GROUPS]
    field_ref, image_ref, scal1_ref = refs[2 * GROUPS : 2 * GROUPS + 3]
    out_weights_ref, out_field_ref = refs[2 * GROUPS + 3 :]
    second = step_length(scal1_ref)
    n_tiles = size.ext // LANES
    for g in range(GROUPS):
        weights = weights_refs[g][...] - second * grad_refs[g][...]
        tiles = [weights[:, e * LANES : (e + 1) * LANES] for e in range(n_tiles)]
        for e in range(n_tiles):
            tile = tiles[e]
            if e + 1 < n_tiles:
                tile = jnp.where(lane(tile.shape) < MARGIN, tiles[e + 1], tile)
            tile = pltpu.roll(tile, LANES - MARGIN, 1)
            start = e * LANES
            width = min(LANES, size.cols - start)
            for r in range(size.rows):
                to = pl.ds(r * size.members + g * size.group, size.group)
                rows = slice(r * size.group, (r + 1) * size.group)
                out_weights_ref[to, start : start + width] = tile[rows, :width]
    field = field_ref[...] - second * image_ref[...]
    start = 0
    for tile, width in share_tiles(size, field):
        for v in range(size.vars):
            rows = slice(v * size.fine_rows, (v + 1) * size.fine_rows)
            out_field_ref[v, :, start : start + width] = tile[rows, :width]
        start += width


def whole():
    return pl.BlockSpec(memory_space=pltpu.VMEM)


def params(limit):
    return pltpu.CompilerParams(vmem_limit_bytes=limit * 1024 * 1024)


def array(*shape):
    return jax.ShapeDtypeStruct(shape, F32)


def call(kernel, outs, *args, scratch=(), flops=0, spaces=None, moved=None, limit=24):
    spaces = spaces or [
        pltpu.MemorySpace.SMEM if arg.ndim == 1 else pltpu.MemorySpace.VMEM for arg in args
    ]
    if moved is None:
        moved = sum(arg.size * arg.dtype.itemsize for arg in args)
    return pl.pallas_call(
        kernel,
        out_shape=outs,
        in_specs=[pl.BlockSpec(memory_space=space) for space in spaces],
        out_specs=jax.tree.map(lambda unused: whole(), outs),
        scratch_shapes=scratch,
        compiler_params=params(limit),
        cost_estimate=pl.CostEstimate(flops=flops, bytes_accessed=moved, transcendentals=0),
    )(*args)


def per_device(mesh, perturbations, control, innovations, thresholds):
    size = Sizes(mesh, perturbations, control)
    n_mem, n_lat, members = size.n_mem, size.n_lat, size.members
    devices = n_mem * n_lat
    pairs = [(i, i ^ 1) for i in range(n_lat)]
    cross = []
    for k in range(n_mem):
        for i in range(n_lat):
            to = (k ^ 1, i) if i in (0, n_lat - 1) else (k, i - 1 if i % 2 == 0 else i + 1)
            cross.append((k * n_lat + i, to[0] * n_lat + to[1]))
    middle_first = sorted(range(1, n_mem), key=lambda d: (d != n_mem // 2, d))
    groups = range(GROUPS)
    slab = array(size.slab, size.ext)
    packed = array(size.packed, LANES)
    part = array(size.part_rows, LANES)
    share = array(size.share_rows, LANES)
    scal = array(devices, LANES)
    field = array(size.list_rows, LANES)
    map_flops = 4 * size.group * size.fine_rows * size.fine_cols * 2 * LANES

    def swap(to_a, to_b):
        return lax.ppermute(to_a, "lat", pairs), lax.ppermute(to_b, ("mem", "lat"), cross)

    def exchange(parts, order):
        return [parts[0]] + [
            lax.ppermute(parts[d], "mem", [(i, i ^ d) for i in range(n_mem)]) for d in order
        ]

    def forward(order, owns, arrived, *first_step):
        shares = len(first_step) > 0
        acc = []
        piece = share if shares else part
        for g in groups:
            last = g == GROUPS - 1
            scratch = [
                pltpu.VMEM((3 * size.slab, size.ext), F32),
                pltpu.VMEM(((size.rows + 2) * size.group, size.ext), F32),
                pltpu.VMEM((size.windows, size.group * size.fine_rows, LANES), F32),
            ]
            if last:
                scratch.append(pltpu.VMEM(field.shape, F32))
                if shares:
                    scratch.append(pltpu.VMEM((n_mem, *piece.shape), F32))
            outs = [piece] * n_mem if last else [field]
            extra = shares and g == 0
            if extra:
                outs.append(share)
                scratch += [pltpu.VMEM(field.shape, F32), pltpu.VMEM((n_mem, *share.shape), F32)]
            acc = call(
                functools.partial(forward_kernel, size, g, shares),
                outs,
                owns[g],
                *arrived[g][::-1],
                resident,
                *acc,
                *(first_step if extra else ()),
                scratch=scratch,
                flops=map_flops,
            )
            if extra:
                *acc, own_share = acc
        acc = exchange(acc, order)
        return (acc, own_share) if shares else acc

    def adjoint(parts, *step):
        later = len(step) > 0
        sent, spread, misfit, whole_field = [], [], None, None
        for g in groups:
            scratch = [
                pltpu.VMEM((size.ext // LANES, size.group * size.fine_rows, LANES), F32),
                pltpu.VMEM(((size.rows + 2) * size.group, size.ext), F32),
                pltpu.VMEM((3 * size.slab, size.ext), F32),
                pltpu.VMEM((size.windows, size.group * size.fine_rows, 2 * FINE), BF16),
            ]
            outs = [packed, packed, slab]
            args = [misfit]
            if g == 0:
                outs += [field, field]
                args = [*parts, *step, innovations, thresholds.reshape(1, size.vars)]
            results = call(
                functools.partial(adjoint_kernel, size, g, later),
                outs,
                resident,
                *args,
                scratch=scratch,
                flops=map_flops,
            )
            sent.append(swap(*results[:2]))
            spread.append(results[2])
            if g == 0:
                misfit = results[3]
                whole_field = results[4]
        return sent, spread, whole_field

    def gradient(arrived, spread, weights, *step):
        later = len(step) > 0
        grads, sent, olds = [], [], []
        for g in groups:
            results = call(
                functools.partial(gradient_kernel, size, later),
                [slab, packed] + ([slab] if later else []),
                spread[g],
                *arrived[g][::-1],
                weights[g],
                *([step[0], step[1][g]] if later else []),
            )
            grads.append(results[0])
            sent.append(results[1])
            olds.append(results[2] if later else weights[g])
        return grads, sent, olds

    def squares(parts, sent):
        return call(
            functools.partial(squares_kernel, n_mem),
            [array(*parts[0].shape), scal],
            *parts,
            *sent,
        )

    def everywhere(tile):
        moved = lax.all_to_all(tile.reshape(devices, 1, LANES), ("mem", "lat"), 0, 0)
        return moved.reshape(devices, LANES)

    def both(sent):
        return [swap(x, x) for x in sent]

    entered = call(
        functools.partial(enter_kernel, size),
        [slab, packed] * GROUPS,
        control.transpose(1, 0, 2).reshape(size.rows * members, size.cols),
    )
    control_own, sent = entered[0::2], entered[1::2]
    copies = min(4, members)
    resident = call(
        load_kernel,
        pltpu.VMEM(perturbations.shape, F32),
        pltpu.with_memory_space_constraint(perturbations, pltpu.HBM),
        scratch=[
            pltpu.VMEM(perturbations.shape, perturbations.dtype),
            pltpu.SemaphoreType.DMA((copies,)),
        ],
        spaces=[pltpu.MemorySpace.HBM],
        flops=2 * map_flops,
    )
    parts = forward(size.far_first, control_own, both(sent))
    field0 = call(functools.partial(total_kernel, n_mem), part, *parts)
    arrived, spread, before = adjoint(exchange([field0] * n_mem, size.far_first))
    grads0, sent, unused = gradient(arrived, spread, control_own)
    parts = forward(middle_first, grads0, both(sent))
    image0, scal0 = squares(parts, sent)
    images = exchange([image0] * n_mem, size.far_first)
    scal0 = everywhere(scal0)
    arrived, spread, image_all = adjoint(images, scal0, before)
    grads1, sent, weights1 = gradient(arrived, spread, control_own, scal0, grads0)
    parts, own_share = forward(middle_first, grads1, both(sent), before, image_all, scal0)
    image1, scal1 = squares(parts, sent)
    scal1 = everywhere(scal1)
    weights, result = call(
        functools.partial(leave_kernel, size),
        [
            array(size.rows * members, size.cols),
            array(size.vars, size.fine_rows, size.share),
        ],
        *weights1,
        *grads1,
        own_share,
        image1,
        scal1,
    )
    return weights.reshape(size.rows, members, size.cols).transpose(1, 0, 2), result


def solution(mesh):
    return jax.shard_map(
        functools.partial(per_device, mesh),
        mesh=mesh,
        in_specs=(P("mem", None, "lat", None), P("mem", "lat", None), P(None, "lat", None), P()),
        out_specs=(P("mem", "lat", None), P(None, "lat", "mem")),
        check_vma=False,
    )
```

```python
import functools

import jax
import jax.numpy as jnp
from jax import lax
from jax.experimental import pallas as pl
from jax.experimental.pallas import tpu as pltpu
from jax.sharding import PartitionSpec as P

RATIO = 4
HALF = 5
STEPS = 2
REACH = HALF + 1
LANES = 128
WIN = 64
MARGIN = 32
FINE = RATIO * WIN
GROUPS = 2
F32 = jnp.float32
BF16 = jnp.bfloat16


def tent(distance):
    return max(0.0, 1.0 - abs(distance) / RATIO)


def smooth(distance):
    return (1.0 - abs(distance) / REACH) / 2 if abs(distance) <= HALF else 0.0


def window_table(fine_axis, width=LANES):
    shape = (FINE, width) if fine_axis == 0 else (width, FINE)
    fine = lax.broadcasted_iota(jnp.int32, shape, fine_axis).astype(F32)
    coarse = lax.broadcasted_iota(jnp.int32, shape, 1 - fine_axis).astype(F32)
    coarse = coarse - (MARGIN + (width - LANES) // 2)
    distance = fine + 0.5 - RATIO * coarse - RATIO / 2
    table = jnp.maximum(0.0, 1.0 - jnp.abs(distance) / RATIO).astype(BF16)
    return jnp.concatenate([table, table], axis=0)


class Sizes:
    def __init__(self, mesh, perturbations, control):
        self.n_mem = mesh.shape["mem"]
        self.n_lat = mesh.shape["lat"]
        self.far_first = range(self.n_mem - 1, 0, -1)
        self.members = control.shape[0]
        self.group = self.members // GROUPS
        self.rows = control.shape[1]
        self.cols = control.shape[2]
        self.vars = perturbations.shape[1]
        self.fine_rows = perturbations.shape[2]
        self.fine_cols = perturbations.shape[3]
        assert self.rows == REACH and self.cols % LANES == WIN
        assert self.members % (8 * GROUPS) == 0 and self.n_lat % 2 == 0
        assert self.fine_rows == RATIO * self.rows and self.fine_cols == RATIO * self.cols
        self.windows = self.cols // WIN
        self.ext = self.cols + 2 * MARGIN
        self.slab = self.rows * self.group
        self.full = self.cols // LANES
        self.packed = self.full * self.slab + self.slab // 2
        self.field_rows = self.vars * self.fine_rows
        self.share = self.fine_cols // self.n_mem
        self.share_full = self.share // LANES
        self.share_rem = self.share % LANES
        self.groups = LANES // self.share_rem if self.share_rem else 1
        self.rem_rows = -(-self.field_rows // 8 // self.groups) * 8 if self.share_rem else 0
        self.share_rows = self.share_full * self.field_rows + self.rem_rows
        self.field_tiles = self.fine_cols // LANES
        self.part_rows = -(-self.field_tiles * self.field_rows // 8 // self.n_mem) * 8
        self.list_rows = self.part_rows * self.n_mem


def lane(shape):
    return lax.broadcasted_iota(jnp.int32, shape, 1)


def half_turn(x):
    return pltpu.roll(x, WIN, 1)


def pack_slab(size, first, last, middle):
    rows = size.slab
    at = lane((rows, LANES))
    pieces = list(middle)
    pieces.append(jnp.where(at < LANES - MARGIN, last, first))
    half = rows // 2
    at = lane((half, LANES))
    inner = (at >= MARGIN) & (at < LANES - MARGIN)
    pieces.append(jnp.where(inner, first[:half], half_turn(first[half:])))
    return pieces


def unpack_slab(size, packed):
    rows = size.slab
    middle = [packed[i * rows : (i + 1) * rows] for i in range(size.full - 1)]
    mixed = packed[(size.full - 1) * rows : size.full * rows]
    rest = packed[size.full * rows :]
    rest = jnp.concatenate([rest, half_turn(rest)], axis=0)
    at = lane((rows, LANES))
    first = jnp.where(at < MARGIN, half_turn(mixed), jnp.where(at < LANES - MARGIN, rest, mixed))
    last = jnp.where(at < LANES - MARGIN, mixed, half_turn(rest))
    return [first] + middle + [last]


def tiles_of(ref, count):
    return [ref[:, i * LANES : (i + 1) * LANES] for i in range(count)]


def put_packed(out, pieces):
    at = 0
    for piece in pieces:
        out[at : at + piece.shape[0], :] = piece
        at += piece.shape[0]


def pack_ref(size, out, tiles):
    put_packed(out, pack_slab(size, tiles[0], tiles[-1], tiles[1:-1]))


def place():
    lat = lax.axis_index("lat")
    odd = lax.rem(lat, 2) == 1
    low = (lat > 0).astype(F32)
    high = (lat < lax.axis_size("lat") - 1).astype(F32)
    return odd, low, high


def sides(a, b):
    odd, low, high = place()
    lower = jnp.where(odd, a, b) * low
    upper = jnp.where(odd, b, a) * high
    return lower, upper


def step_length(scal_ref):
    total = jnp.sum(scal_ref[...], axis=0, keepdims=True)
    at = lane(total.shape)
    grad_sq = jnp.sum(jnp.where(at == 0, total, 0.0), axis=1, keepdims=True)
    image_sq = jnp.sum(jnp.where(at == 1, total, 0.0), axis=1, keepdims=True)
    return grad_sq / (grad_sq + image_sq)


def enter_kernel(size, control_ref, *outs):
    for g in range(GROUPS):
        own_ref, packed_ref = outs[2 * g : 2 * g + 2]
        x = jnp.concatenate(
            [
                control_ref[pl.ds(r * size.members + g * size.group, size.group), :]
                for r in range(size.rows)
            ],
            axis=0,
        )
        own_ref[...] = jnp.concatenate([x[:, size.cols - MARGIN :], x, x[:, :MARGIN]], axis=1)
        pack_ref(size, packed_ref, tiles_of(own_ref, size.ext // LANES))


def load_kernel(pert_ref, out_ref, held_ref, sems):
    count = sems.shape[0]
    part = pert_ref.shape[0] // count
    copies = [
        pltpu.make_async_copy(
            pert_ref.at[pl.ds(i * part, part)], held_ref.at[pl.ds(i * part, part)], sems.at[i]
        )
        for i in range(count)
    ]
    for copy in copies:
        copy.start()
    for i, copy in enumerate(copies):
        copy.wait()

        def widen(m, unused):
            for v in range(pert_ref.shape[1]):
                out_ref[m, v] = held_ref[m, v].astype(F32)
            return unused

        lax.fori_loop(i * part, (i + 1) * part, widen, 0)


def forward_kernel(size, g, shares, own_ref, b_ref, a_ref, pert_ref, *rest):
    rest = list(rest)
    start_ref = rest.pop(0) if g else None
    last = g == GROUPS - 1
    extra = shares and g == 0
    if extra:
        sources = [rest.pop(0) for i in range(3)]
    outs = [rest.pop(0) for i in range(size.n_mem if last else 1)]
    if extra:
        own_share_kernel(size, *sources, rest.pop(0), *rest[-2:])
    ext_ref, coarse_ref, rows_ref = rest[:3]
    acc_ref = rest[3] if last else outs[0]
    members = size.group
    n_tiles = size.ext // LANES
    fine_rows = size.fine_rows

    unused, low, high = place()
    lower, upper = sides(a_ref[...], b_ref[...])
    lower = unpack_slab(size, lower)
    upper = unpack_slab(size, upper)
    n = size.slab
    for e in range(n_tiles):
        cut = slice(e * LANES, (e + 1) * LANES)
        ext_ref[0:n, cut] = lower[e]
        ext_ref[n : 2 * n, cut] = own_ref[:, cut]
        ext_ref[2 * n : 3 * n, cut] = upper[e]
    for e in range(n_tiles):
        cut = slice(e * LANES, (e + 1) * LANES)
        for at in range(0, members, 8):
            held = [
                ext_ref[k * members + at : k * members + at + 8, cut] for k in range(3 * REACH)
            ]
            for j in range(size.rows + 2):
                total = None
                for k in range(3 * REACH):
                    weight = smooth(j - 1 - (k - REACH))
                    if weight:
                        term = held[k] * weight
                        total = term if total is None else total + term
                if j == 0:
                    total = total * low
                if j == size.rows + 1:
                    total = total * high
                coarse_ref[j * members + at : j * members + at + 8, cut] = total
    for t in range(size.windows):
        e = t // 2
        held = []
        for j in range(size.rows + 2):
            at = slice(j * members, (j + 1) * members)
            value = coarse_ref[at, e * LANES : (e + 1) * LANES]
            if t % 2:
                other = coarse_ref[at, (e + 1) * LANES : (e + 2) * LANES]
                value = half_turn(jnp.where(lane(value.shape) < WIN, other, value))
            held.append(value)
        for i in range(fine_rows):
            total = None
            for j in range(size.rows + 2):
                weight = tent(i + 0.5 - RATIO * (j - 1) - RATIO / 2)
                if weight:
                    term = held[j] * weight
                    total = term if total is None else total + term
            rows_ref[t, pl.ds(i, members, stride=fine_rows), :] = total
    table = window_table(1)
    if g:
        acc_ref[...] = start_ref[...]
    else:
        acc_ref[...] = jnp.zeros_like(acc_ref)
    for t in range(size.windows):
        x = rows_ref[t]
        head = x.astype(BF16)
        tail = (x - head.astype(F32)).astype(BF16)
        refined = jnp.dot(
            jnp.concatenate([head, tail], axis=1), table, preferred_element_type=F32
        )
        for e in range(t * FINE // LANES, (t + 1) * FINE // LANES):
            cut = slice(e * LANES, (e + 1) * LANES)
            here = slice(e * LANES - t * FINE, (e + 1) * LANES - t * FINE)
            rows = [
                pl.ds(e * size.field_rows + v * fine_rows, fine_rows)
                for v in range(size.vars)
            ]
            totals = [acc_ref[at, :] for at in rows]
            for m in range(members):
                value = refined[m * fine_rows : (m + 1) * fine_rows, here]
                for v in range(size.vars):
                    pert = pert_ref[g * members + m, v, :, cut]
                    totals[v] = totals[v] + pert * value
            for v in range(size.vars):
                acc_ref[rows[v], :] = totals[v]
    if not last:
        return
    mine = lax.axis_index("mem")
    if shares:
        parts_ref = rest[4]
        for q in range(size.n_mem):
            put_share(size, parts_ref.at[q], acc_ref, q * size.share)
        for d in range(size.n_mem):
            outs[d][...] = parts_ref[mine ^ d]
    else:
        for d in range(size.n_mem):
            first = pl.multiple_of((mine ^ d) * size.part_rows, 8)
            outs[d][...] = acc_ref[pl.ds(first, size.part_rows), :]


def field_tile(size, list_ref, start):
    e, shift = start // LANES, start % LANES
    rows = size.field_rows
    tile = list_ref[e * rows : (e + 1) * rows, :]
    if shift == 0:
        return tile
    if e + 1 < size.field_tiles:
        other = list_ref[(e + 1) * rows : (e + 2) * rows, :]
        tile = jnp.where(lane(tile.shape) < shift, other, tile)
    return pltpu.roll(tile, LANES - shift, 1)


def put_share(size, out, list_ref, start):
    rows = size.field_rows
    for j in range(size.share_full):
        out[j * rows : (j + 1) * rows, :] = field_tile(size, list_ref, start + j * LANES)
    if size.share_rem:
        tile = field_tile(size, list_ref, start + size.share_full * LANES)
        tile = jnp.where(lane(tile.shape) < size.share_rem, tile, 0.0)
        missing = size.rem_rows * size.groups - rows
        if missing:
            tile = jnp.concatenate([tile, jnp.zeros((missing, LANES), F32)], axis=0)
        total = None
        for g in range(size.groups):
            term = tile[g * size.rem_rows : (g + 1) * size.rem_rows]
            if g:
                term = pltpu.roll(term, g * size.share_rem, 1)
            total = term if total is None else total + term
        out[size.share_full * rows :, :] = total


def share_tiles(size, part):
    rows = size.field_rows
    tiles = [(part[j * rows : (j + 1) * rows], LANES) for j in range(size.share_full)]
    if size.share_rem:
        rest = part[size.share_full * rows :]
        stack = [rest]
        for g in range(1, size.groups):
            stack.append(pltpu.roll(rest, LANES - g * size.share_rem, 1))
        tiles.append((jnp.concatenate(stack, axis=0)[:rows], size.share_rem))
    return tiles


def total_kernel(count, *refs):
    parts, out_ref = refs[:count], refs[count]
    total = parts[0][...]
    for part in parts[1:]:
        total = total + part[...]
    out_ref[...] = total


def squares_kernel(count, *refs):
    parts, grads = refs[:count], refs[count : count + GROUPS]
    out_ref, scal_ref = refs[count + GROUPS :]
    total = parts[0][...]
    for part in parts[1:]:
        total = total + part[...]
    out_ref[...] = total
    image_sq = jnp.sum(total * total)
    grad_sq = sum(jnp.sum(grad[...] * grad[...]) for grad in grads)
    at = lane(scal_ref.shape)
    scal_ref[...] = jnp.where(at == 0, grad_sq, jnp.where(at == 1, image_sq, 0.0))


def misfit_of(size, parts, before_ref, scal_ref, innov_ref, limit_ref, list_ref, misfit_ref):
    fine_rows = size.fine_rows
    mine = lax.axis_index("mem")
    for i, d in enumerate((0, *size.far_first)):
        first = pl.multiple_of((mine ^ d) * size.part_rows, 8)
        list_ref[pl.ds(first, size.part_rows), :] = parts[i][...]
    if before_ref is not None:
        length = step_length(scal_ref)
    for e in range(size.field_tiles):
        cut = slice(e * LANES, (e + 1) * LANES)
        for v in range(size.vars):
            at = pl.ds(e * size.field_rows + v * fine_rows, fine_rows)
            value = list_ref[at, :]
            if before_ref is not None:
                value = before_ref[at, :] - length * value
            limit = limit_ref[:, v : v + 1]
            misfit_ref[at, :] = jnp.clip(value - innov_ref[v, :, cut], -limit, limit)


def adjoint_kernel(size, g, later, *refs):
    refs = list(refs)
    pert_ref = refs.pop(0)
    if g == 0:
        parts = [refs.pop(0) for i in range(size.n_mem)]
        scal_ref, before_ref = (refs.pop(0), refs.pop(0)) if later else (None, None)
        innov_ref, limit_ref = refs.pop(0), refs.pop(0)
    else:
        misfit_ref = refs.pop(0)
    a_ref, b_ref, own_ref = refs[:3]
    refs = refs[3:]
    if g == 0:
        misfit_ref = refs.pop(0)
        list_ref = refs.pop(0)
    cols_ref, coarse_ref, spread_ref, held_ref = refs[:4]
    members = size.group
    n_tiles = size.ext // LANES
    fine_rows = size.fine_rows
    if g == 0:
        misfit_of(size, parts, before_ref, scal_ref, innov_ref, limit_ref, list_ref, misfit_ref)
    tables = [window_table(0), window_table(0, 2 * LANES)]

    def weighted(t):
        cut = slice(t * FINE, (t + 1) * FINE)
        tiles = range(t * FINE // LANES, (t + 1) * FINE // LANES)
        mis = [
            jnp.concatenate(
                [
                    misfit_ref[pl.ds(e * size.field_rows + v * fine_rows, fine_rows), :]
                    for e in tiles
                ],
                axis=1,
            )
            for v in range(size.vars)
        ]
        rows = []
        for m in range(members):
            total = pert_ref[g * members + m, 0, :, cut] * mis[0]
            for v in range(1, size.vars):
                total = total + pert_ref[g * members + m, v, :, cut] * mis[v]
            rows.append(total)
        x = jnp.concatenate(rows, axis=0)
        head = x.astype(BF16)
        tail = (x - head.astype(F32)).astype(BF16)
        held_ref[t, :, :FINE] = head
        held_ref[t, :, FINE:] = tail

    def place_columns(t):
        columns = jnp.dot(held_ref[t], tables[t % 2], preferred_element_type=F32)
        e = t // 2
        if t % 2 == 0:
            cols_ref[e] = cols_ref[e] + columns if t else columns
        else:
            cols_ref[e] = cols_ref[e] + columns[:, :LANES]
            cols_ref[e + 1] = columns[:, LANES:]

    weighted(0)
    for t in range(size.windows):
        if t + 1 < size.windows:
            weighted(t + 1)
        place_columns(t)
    odd, low, high = place()
    for e in range(n_tiles):
        cut = slice(e * LANES, (e + 1) * LANES)
        sums = [None] * (size.rows + 2)
        for i in range(fine_rows):
            value = cols_ref[e, pl.ds(i, members, stride=fine_rows), :]
            for j in range(size.rows + 2):
                weight = tent(i + 0.5 - RATIO * (j - 1) - RATIO / 2)
                if weight:
                    term = value * weight
                    sums[j] = term if sums[j] is None else sums[j] + term
        sums[0] = sums[0] * low
        sums[-1] = sums[-1] * high
        for j in range(size.rows + 2):
            coarse_ref[j * members : (j + 1) * members, cut] = sums[j]
    head = coarse_ref[:, 0:LANES]
    tail = coarse_ref[:, (n_tiles - 1) * LANES :]
    at = lane(head.shape)
    turned_head, turned_tail = half_turn(head), half_turn(tail)
    coarse_ref[:, 0:LANES] = head + jnp.where(at < WIN, turned_tail, 0.0)
    coarse_ref[:, (n_tiles - 1) * LANES :] = tail + jnp.where(at >= WIN, turned_head, 0.0)
    for e in range(n_tiles):
        cut = slice(e * LANES, (e + 1) * LANES)
        for at in range(0, members, 8):
            held = [
                coarse_ref[j * members + at : j * members + at + 8, cut]
                for j in range(size.rows + 2)
            ]
            for k in range(3 * REACH):
                total = None
                for j in range(size.rows + 2):
                    weight = smooth(j - 1 - (k - REACH))
                    if weight:
                        term = held[j] * weight
                        total = term if total is None else total + term
                spread_ref[k * members + at : k * members + at + 8, cut] = total
    n = size.slab

    def packed_of(part):
        tiles = [
            spread_ref[part * n : (part + 1) * n, e * LANES : (e + 1) * LANES]
            for e in range(n_tiles)
        ]
        return pack_slab(size, tiles[0], tiles[-1], tiles[1:-1])

    lower, upper = packed_of(0), packed_of(2)
    own_ref[...] = spread_ref[n : 2 * n, :]
    put_packed(a_ref, [jnp.where(odd, x, y) for x, y in zip(lower, upper)])
    put_packed(b_ref, [jnp.where(odd, y, x) for x, y in zip(lower, upper)])


def gradient_kernel(size, later, *refs):
    refs = list(refs)
    own_ref, b_ref, a_ref, weights_ref = refs[:4]
    refs = refs[4:]
    weights = weights_ref[...]
    if later:
        scal_ref, before_ref = refs.pop(0), refs.pop(0)
        weights = weights - step_length(scal_ref) * before_ref[...]
    grad_ref, packed_ref = refs[:2]
    if later:
        refs[2][...] = weights
    lower, upper = sides(a_ref[...], b_ref[...])
    arrived = unpack_slab(size, lower + upper)
    for e in range(size.ext // LANES):
        cut = slice(e * LANES, (e + 1) * LANES)
        grad_ref[:, cut] = weights[:, cut] + own_ref[:, cut] + arrived[e]
    pack_ref(size, packed_ref, tiles_of(grad_ref, size.ext // LANES))


def own_share_kernel(size, before_ref, image_ref, scal_ref, out_ref, list_ref, shares_ref):
    list_ref[...] = before_ref[...] - step_length(scal_ref) * image_ref[...]
    for q in range(size.n_mem):
        put_share(size, shares_ref.at[q], list_ref, q * size.share)
    out_ref[...] = shares_ref[lax.axis_index("mem")]


def leave_kernel(size, *refs):
    weights_refs, grad_refs = refs[:GROUPS], refs[GROUPS : 2 * GROUPS]
    field_ref, image_ref, scal1_ref = refs[2 * GROUPS : 2 * GROUPS + 3]
    out_weights_ref, out_field_ref = refs[2 * GROUPS + 3 :]
    second = step_length(scal1_ref)
    n_tiles = size.ext // LANES
    for g in range(GROUPS):
        weights = weights_refs[g][...] - second * grad_refs[g][...]
        tiles = [weights[:, e * LANES : (e + 1) * LANES] for e in range(n_tiles)]
        for e in range(n_tiles):
            tile = tiles[e]
            if e + 1 < n_tiles:
                tile = jnp.where(lane(tile.shape) < MARGIN, tiles[e + 1], tile)
            tile = pltpu.roll(tile, LANES - MARGIN, 1)
            start = e * LANES
            width = min(LANES, size.cols - start)
            for r in range(size.rows):
                to = pl.ds(r * size.members + g * size.group, size.group)
                rows = slice(r * size.group, (r + 1) * size.group)
                out_weights_ref[to, start : start + width] = tile[rows, :width]
    field = field_ref[...] - second * image_ref[...]
    start = 0
    for tile, width in share_tiles(size, field):
        for v in range(size.vars):
            rows = slice(v * size.fine_rows, (v + 1) * size.fine_rows)
            out_field_ref[v, :, start : start + width] = tile[rows, :width]
        start += width


def whole():
    return pl.BlockSpec(memory_space=pltpu.VMEM)


def params(limit):
    return pltpu.CompilerParams(vmem_limit_bytes=limit * 1024 * 1024)


def array(*shape):
    return jax.ShapeDtypeStruct(shape, F32)


def call(kernel, outs, *args, scratch=(), flops=0, spaces=None, moved=None, limit=24):
    spaces = spaces or [
        pltpu.MemorySpace.SMEM if arg.ndim == 1 else pltpu.MemorySpace.VMEM for arg in args
    ]
    if moved is None:
        moved = sum(arg.size * arg.dtype.itemsize for arg in args)
    return pl.pallas_call(
        kernel,
        out_shape=outs,
        in_specs=[pl.BlockSpec(memory_space=space) for space in spaces],
        out_specs=jax.tree.map(lambda unused: whole(), outs),
        scratch_shapes=scratch,
        compiler_params=params(limit),
        cost_estimate=pl.CostEstimate(flops=flops, bytes_accessed=moved, transcendentals=0),
    )(*args)


def per_device(mesh, perturbations, control, innovations, thresholds):
    size = Sizes(mesh, perturbations, control)
    n_mem, n_lat, members = size.n_mem, size.n_lat, size.members
    devices = n_mem * n_lat
    pairs = [(i, i ^ 1) for i in range(n_lat)]
    cross = []
    for k in range(n_mem):
        for i in range(n_lat):
            to = (k ^ 1, i) if i in (0, n_lat - 1) else (k, i - 1 if i % 2 == 0 else i + 1)
            cross.append((k * n_lat + i, to[0] * n_lat + to[1]))
    middle_first = sorted(range(1, n_mem), key=lambda d: (d != n_mem // 2, d))
    groups = range(GROUPS)
    slab = array(size.slab, size.ext)
    packed = array(size.packed, LANES)
    part = array(size.part_rows, LANES)
    share = array(size.share_rows, LANES)
    scal = array(devices, LANES)
    field = array(size.list_rows, LANES)
    map_flops = 4 * size.group * size.fine_rows * size.fine_cols * 2 * LANES

    def swap(to_a, to_b):
        return lax.ppermute(to_a, "lat", pairs), lax.ppermute(to_b, ("mem", "lat"), cross)

    def exchange(parts, order):
        return [parts[0]] + [
            lax.ppermute(parts[d], "mem", [(i, i ^ d) for i in range(n_mem)]) for d in order
        ]

    def forward(order, owns, arrived, *first_step):
        shares = len(first_step) > 0
        acc = []
        piece = share if shares else part
        for g in groups:
            last = g == GROUPS - 1
            scratch = [
                pltpu.VMEM((3 * size.slab, size.ext), F32),
                pltpu.VMEM(((size.rows + 2) * size.group, size.ext), F32),
                pltpu.VMEM((size.windows, size.group * size.fine_rows, LANES), F32),
            ]
            if last:
                scratch.append(pltpu.VMEM(field.shape, F32))
                if shares:
                    scratch.append(pltpu.VMEM((n_mem, *piece.shape), F32))
            outs = [piece] * n_mem if last else [field]
            extra = shares and g == 0
            if extra:
                outs.append(share)
                scratch += [pltpu.VMEM(field.shape, F32), pltpu.VMEM((n_mem, *share.shape), F32)]
            acc = call(
                functools.partial(forward_kernel, size, g, shares),
                outs,
                owns[g],
                *arrived[g][::-1],
                resident,
                *acc,
                *(first_step if extra else ()),
                scratch=scratch,
                flops=map_flops,
            )
            if extra:
                *acc, own_share = acc
        acc = exchange(acc, order)
        return (acc, own_share) if shares else acc

    def adjoint(parts, *step):
        later = len(step) > 0
        sent, spread, misfit, whole_field = [], [], None, None
        for g in groups:
            scratch = [
                pltpu.VMEM((size.ext // LANES, size.group * size.fine_rows, LANES), F32),
                pltpu.VMEM(((size.rows + 2) * size.group, size.ext), F32),
                pltpu.VMEM((3 * size.slab, size.ext), F32),
                pltpu.VMEM((size.windows, size.group * size.fine_rows, 2 * FINE), BF16),
            ]
            outs = [packed, packed, slab]
            args = [misfit]
            if g == 0:
                outs += [field, field]
                args = [*parts, *step, innovations, thresholds.reshape(1, size.vars)]
            results = call(
                functools.partial(adjoint_kernel, size, g, later),
                outs,
                resident,
                *args,
                scratch=scratch,
                flops=map_flops,
            )
            sent.append(swap(*results[:2]))
            spread.append(results[2])
            if g == 0:
                misfit = results[3]
                whole_field = results[4]
        return sent, spread, whole_field

    def gradient(arrived, spread, weights, *step):
        later = len(step) > 0
        grads, sent, olds = [], [], []
        for g in groups:
            results = call(
                functools.partial(gradient_kernel, size, later),
                [slab, packed] + ([slab] if later else []),
                spread[g],
                *arrived[g][::-1],
                weights[g],
                *([step[0], step[1][g]] if later else []),
            )
            grads.append(results[0])
            sent.append(results[1])
            olds.append(results[2] if later else weights[g])
        return grads, sent, olds

    def squares(parts, sent):
        return call(
            functools.partial(squares_kernel, n_mem),
            [array(*parts[0].shape), scal],
            *parts,
            *sent,
        )

    def everywhere(tile):
        moved = lax.all_to_all(tile.reshape(devices, 1, LANES), ("mem", "lat"), 0, 0)
        return moved.reshape(devices, LANES)

    def both(sent):
        return [swap(x, x) for x in sent]

    entered = call(
        functools.partial(enter_kernel, size),
        [slab, packed] * GROUPS,
        control.transpose(1, 0, 2).reshape(size.rows * members, size.cols),
    )
    control_own, sent = entered[0::2], entered[1::2]
    copies = min(8, members)
    resident = call(
        load_kernel,
        pltpu.VMEM(perturbations.shape, F32),
        pltpu.with_memory_space_constraint(perturbations, pltpu.HBM),
        scratch=[
            pltpu.VMEM(perturbations.shape, perturbations.dtype),
            pltpu.SemaphoreType.DMA((copies,)),
        ],
        spaces=[pltpu.MemorySpace.HBM],
        flops=2 * map_flops,
    )
    parts = forward(size.far_first, control_own, both(sent))
    field0 = call(functools.partial(total_kernel, n_mem), part, *parts)
    arrived, spread, before = adjoint(exchange([field0] * n_mem, size.far_first))
    grads0, sent, unused = gradient(arrived, spread, control_own)
    parts = forward(middle_first, grads0, both(sent))
    image0, scal0 = squares(parts, sent)
    images = exchange([image0] * n_mem, size.far_first)
    scal0 = everywhere(scal0)
    arrived, spread, image_all = adjoint(images, scal0, before)
    grads1, sent, weights1 = gradient(arrived, spread, control_own, scal0, grads0)
    parts, own_share = forward(middle_first, grads1, both(sent), before, image_all, scal0)
    image1, scal1 = squares(parts, sent)
    scal1 = everywhere(scal1)
    weights, result = call(
        functools.partial(leave_kernel, size),
        [
            array(size.rows * members, size.cols),
            array(size.vars, size.fine_rows, size.share),
        ],
        *weights1,
        *grads1,
        own_share,
        image1,
        scal1,
    )
    return weights.reshape(size.rows, members, size.cols).transpose(1, 0, 2), result


def solution(mesh):
    return jax.shard_map(
        functools.partial(per_device, mesh),
        mesh=mesh,
        in_specs=(P("mem", None, "lat", None), P("mem", "lat", None), P(None, "lat", None), P()),
        out_specs=(P("mem", "lat", None), P(None, "lat", "mem")),
        check_vma=False,
    )
```
